512 devices in a mesh: row: 16 (over y, core), col: 32 (over z, x).
Axes of the slice: x: 4, y: 8, z: 8, core: 2. Of those that a mesh axis runs over, the one named last changes fastest.
Arguments:
- matrix: float32 [8192, 8192], P('row', 'col'), as said below
Outputs:
- panels: float32 [8192, 512], P(('row', 'col'))
- trailing_part: float32 [8192, 8192], P('row', 'col')
Inputs may be any that keep to these rules, and one draw needn't show every extreme that they name: matrix is symmetric and positive definite.
All inputs are finite; a program needn't handle non-finite values.
Results may differ from the reference program's by a relative error of at most 0.00007.
Values sent between devices are 32-bit elements; how exact they have to be, the bound alone decides.
No kernel may reach another device: no remote copies, remote signals or barrier semaphores. Data moves between devices by JAX's collectives and lax.ppermute only.
A program may use at most 64 MiB of HBM per device.

```python
import math
import jax
import jax.numpy as jnp
from jax import lax

NB = 256
M = 8192


def draw_matrix(key, part):
    keys = jax.random.split(jax.random.fold_in(key, 11), 4)
    noise = jnp.clip(jax.random.normal(keys[0], (M, M), jnp.float32), -4.0, 4.0)
    ridge = jax.random.uniform(keys[1], (M,), jnp.float32, 3.0, 4.0)
    scales = jax.random.uniform(keys[2], (M,), jnp.float32, 0.5, 1.5)
    reach = NB / 8.0
    places = jnp.arange(M, dtype=jnp.float32) + jax.random.uniform(keys[3], (M,), jnp.float32, -0.5, 0.5)
    sym = jnp.clip((noise + noise.T) * 0.70710677, -4.0, 4.0)
    spacing = (places[:, None] - places[None, :]) / reach
    kernel = 2.0 * math.sqrt(M) * scales[:, None] * scales[None, :] * jnp.exp(-0.5 * spacing * spacing)
    index_rows = jnp.arange(M)[:, None]
    index_cols = jnp.arange(M)[None, :]
    diag_values = ridge * math.sqrt(M)
    return (jnp.where(index_rows == index_cols, diag_values[:, None], sym) + kernel).astype(jnp.float32)


def setup_inputs(seed: int = 0) -> dict:
    key_of = jax.random.split(jax.random.key(seed), 2)
    return {
        "matrix": draw_matrix(jax.random.fold_in(key_of[1], 71), 0),
    }


def one_panel(square, width):
    diag = jnp.linalg.cholesky(square[:width, :width])
    below = lax.linalg.triangular_solve(diag, square[width:, :width], left_side=False, lower=True, transpose_a=True)
    rest = square[width:, width:] - jnp.dot(below.astype(jnp.float32), below.T.astype(jnp.float32), precision=lax.Precision.HIGHEST, preferred_element_type=jnp.float32)
    return (diag, below, rest)

def reference(matrix):
    first_diag, first_below, schur = one_panel(matrix, NB)
    second_diag, second_below, trailing = one_panel(schur, NB)
    panels = jnp.zeros((M, 2 * NB), jnp.float32)
    panels = panels.at[:NB, :NB].set(first_diag)
    panels = panels.at[NB:, :NB].set(first_below)
    panels = panels.at[NB:2 * NB, NB:2 * NB].set(second_diag)
    panels = panels.at[2 * NB:, NB:2 * NB].set(second_below)
    trailing_part = jnp.zeros((M, M), jnp.float32)
    trailing_part = trailing_part.at[2 * NB:, 2 * NB:].set(trailing)
    return (panels, trailing_part)
```

```python
import jax, jax.numpy as jnp
from jax import lax
from jax.experimental import pallas as pl
from jax.experimental.pallas import tpu as pltpu
from jax.sharding import PartitionSpec as P

HI = lax.Precision.HIGHEST
B = 128
S8 = 8

def rep(x):
    return jnp.broadcast_to(x, (S8, B))

def factor_tile(d_ref, m_ref, lt_ref):
    tiles = B // S8
    for b in range(tiles):
        rows = pl.ds(b * S8, S8)
        d = d_ref[rows, :]
        m = m_ref[rows, :]
        cols = [rep(d[:, b * S8 + k : b * S8 + k + 1]) for k in range(S8)]
        s = {}
        for i in range(S8):
            for k in range(i, S8):
                s[i, k] = rep(cols[k][i : i + 1, :])
        rd = [rep(d[j : j + 1, :]) for j in range(S8)]
        rm = [rep(m[j : j + 1, :]) for j in range(S8)]
        u, qd, qm, scale = {}, [], [], []
        for j in range(S8):
            inv = 1.0 / s[j, j]
            scale.append(lax.rsqrt(s[j, j]))
            for k in range(j + 1, S8):
                u[j, k] = s[j, k] * inv
            for i in range(j + 1, S8):
                for k in range(i, S8):
                    s[i, k] = s[i, k] - s[j, i] * u[j, k]
            qd.append(rd[j] * inv)
            qm.append(rm[j] * inv)
            for k in range(j + 1, S8):
                rd[k] = rd[k] - s[j, k] * qd[j]
                rm[k] = rm[k] - s[j, k] * qm[j]
        for t in range(b + 1, tiles):
            at = pl.ds(t * S8, S8)
            dt = d_ref[at, :]
            mt = m_ref[at, :]
            c = [rep(dt[:, b * S8 + k : b * S8 + k + 1]) for k in range(S8)]
            for j in range(S8):
                for k in range(j + 1, S8):
                    c[k] = c[k] - c[j] * u[j, k]
            for j in range(S8):
                dt = dt - c[j] * qd[j]
                mt = mt - c[j] * qm[j]
            d_ref[at, :] = dt
            m_ref[at, :] = mt
        sub = lax.broadcasted_iota(jnp.int32, (S8, B), 0)
        od, om = rd[0] * scale[0], rm[0] * scale[0]
        for j in range(1, S8):
            od = jnp.where(sub == j, rd[j] * scale[j], od)
            om = jnp.where(sub == j, rm[j] * scale[j], om)
        lt_ref[rows, :] = od
        m_ref[rows, :] = om

def dot(a, b, dims=((1,), (0,))):
    return lax.dot_general(a, b, (dims, ((), ())), precision=HI, preferred_element_type=jnp.float32)

BLOCKS = tuple((i, j) for i in range(4) for j in range(i + 1))


def chol_kernel(g_ref, l_ref, inv_ref, s_ref, d_ref, m_ref, lt_ref):
    n = l_ref.shape[0]
    s_ref[...] = jnp.zeros((n, n), jnp.float32)
    for at, (i, j) in enumerate(BLOCKS):
        s_ref[i * B : (i + 1) * B, j * B : (j + 1) * B] = g_ref[:, at].reshape(B, B)
    ri = lax.broadcasted_iota(jnp.int32, (n, n), 0)
    ci = lax.broadcasted_iota(jnp.int32, (n, n), 1)
    inv_ref[...] = jnp.where(ri == ci, 1.0, 0.0).astype(jnp.float32)
    l_ref[...] = jnp.zeros((n, n), jnp.float32)
    r128 = lax.broadcasted_iota(jnp.int32, (B, B), 0)
    c128 = lax.broadcasted_iota(jnp.int32, (B, B), 1)
    eye = jnp.where(r128 == c128, 1.0, 0.0).astype(jnp.float32)
    rn = lax.broadcasted_iota(jnp.int32, (n, B), 0)

    def step(k, carry):
        off = pl.multiple_of(k * B, B)
        d_ref[...] = s_ref[pl.ds(off, B), pl.ds(off, B)]
        m_ref[...] = eye
        factor_tile(d_ref, m_ref, lt_ref)
        inv = m_ref[...]
        lower = jnp.where(r128 >= c128, lt_ref[...].T, 0.0)
        below = dot(s_ref[:, pl.ds(off, B)], inv, ((1,), (1,)))
        below = jnp.where(rn >= off + B, below, 0.0)
        l_ref[:, pl.ds(off, B)] = below
        l_ref[pl.ds(off, B), pl.ds(off, B)] = lower
        mine = dot(inv, inv_ref[pl.ds(off, B), :])
        s_ref[...] -= dot(below, below, ((1,), (1,)))
        inv_ref[...] -= dot(below, mine)
        inv_ref[pl.ds(off, B), :] = mine
        return carry

    lax.fori_loop(0, n // B, step, 0)


def whole():
    return pl.BlockSpec(memory_space=pltpu.VMEM)


def chol(gathered):
    n = 4 * B
    out = jax.ShapeDtypeStruct((n, n), jnp.float32)
    return pl.pallas_call(
        chol_kernel,
        out_shape=(out, out),
        in_specs=[whole()],
        out_specs=(whole(), whole()),
        scratch_shapes=[pltpu.VMEM((n, n), jnp.float32)] + [pltpu.VMEM((B, B), jnp.float32)] * 3,
        compiler_params=pltpu.CompilerParams(vmem_limit_bytes=40 * 2**20),
    )(gathered)


def final_kernel(x_ref, mine_ref, far_ref, top_ref, l_ref, inv_ref, panel_ref, out_ref, u_ref, f_ref):
    row, col = lax.axis_index("row"), lax.axis_index("col")
    z = col // 8
    inv = inv_ref[...]
    top = jnp.concatenate([top_ref[:, i].reshape(B, -1) for i in range(4)], axis=0)
    u_ref[...] = dot(inv, top)
    for s in range(4):
        piece = mine_ref[...] if s == 0 else far_ref[s - 1]
        at = pl.multiple_of(lax.rem(z + 4 - s, 4) * B, B)
        f_ref[pl.ds(at, B), :] = dot(piece, inv, ((1,), (1,)))

    @pl.when(row == 0)
    def _():
        f_ref[...] = l_ref[...]

    panel_ref[...] = f_ref[pl.ds(pl.multiple_of(col * 16, 16), 16), :]
    live = jnp.logical_and(row > 0, col > 1)

    @pl.when(live)
    def _():
        out_ref[...] = x_ref[...] - dot(f_ref[...], u_ref[...])

    @pl.when(jnp.logical_not(live))
    def _():
        out_ref[...] = jnp.zeros_like(out_ref)


def final(x, mine, far, top, lower, inv):
    return pl.pallas_call(
        final_kernel,
        out_shape=(
            jax.ShapeDtypeStruct((16, 512), jnp.float32),
            jax.ShapeDtypeStruct((512, 256), jnp.float32),
        ),
        in_specs=[whole()] * 6,
        out_specs=(whole(), whole()),
        scratch_shapes=[pltpu.VMEM((512, 256), jnp.float32), pltpu.VMEM((512, 512), jnp.float32)],
        compiler_params=pltpu.CompilerParams(vmem_limit_bytes=40 * 2**20),
    )(x, mine, far, top, lower, inv)


def on_device(x):
    col = lax.axis_index("col")
    first = col == 0
    z = col // 8

    def send(v, pairs):
        return lax.ppermute(v, "col", pairs)

    part = [x[q * B : (q + 1) * B] for q in range(4)]
    moved = [send(part[q], [(0, 8 * q), (1, 8 * q + 1)]) for q in range(1, 4)]
    quarter = jnp.where(z == 0, part[0], moved[0] + moved[1] + moved[2])
    quarter = jnp.where(col % 8 < 2, quarter, 0.0)
    planes = range(0, 32, 8)
    quarter += send(quarter, [(p + i, p + i + 4) for p in planes for i in (0, 1)])
    quarter += send(quarter, [(p + i, p + i + 2) for p in planes for i in (0, 1, 4, 5)])
    other = send(quarter, [(i, i ^ 1) for i in range(32)])
    even = col % 2 == 0
    mine = jnp.concatenate(
        [jnp.where(even, quarter, other), jnp.where(even, other, quarter)], axis=1
    )
    far = jnp.stack([send(mine, [(i, (i + 8 * s) % 32) for i in range(32)]) for s in (1, 2, 3)])

    split = x.reshape(4, 16, 8, 256).transpose(1, 0, 2, 3)
    piece = lax.all_to_all(split, "row", 0, 0)[0]
    swapped = send(piece, [(0, 1), (1, 0)])
    left = jnp.where(first, piece, swapped)
    right = jnp.where(first, swapped, piece)
    groups = []
    for i, j in BLOCKS:
        side = left if j < 2 else right
        groups.append(side[i, :, (j % 2) * B : (j % 2 + 1) * B])
    packed = jnp.where(col < 2, jnp.stack(groups), 0.0)
    packed += sum(send(packed, [(0, 8 * q), (1, 8 * q + 1)]) for q in range(1, 4))
    packed += sum(send(packed, [(p + i, p + i + s) for p in planes for i in (0, 1)]) for s in (2, 4, 6))
    gathered = lax.all_gather(packed, "row")
    lower, inv = chol(gathered)
    top = lax.all_gather(piece, "row")
    return final(x, mine, far, top, lower, inv)


def solution(mesh):
    return jax.shard_map(
        on_device,
        mesh=mesh,
        in_specs=(P("row", "col"),),
        out_specs=(P(("row", "col"), None), P("row", "col")),
        check_vma=False,
    )
```

```python
import functools

import jax, jax.numpy as jnp
from jax import lax
from jax.experimental import pallas as pl
from jax.experimental.pallas import tpu as pltpu
from jax.sharding import PartitionSpec as P

HI = lax.Precision.HIGHEST
B = 128
S8 = 8

def rep(x):
    return jnp.broadcast_to(x, (S8, B))

def factor_tile(d_ref, m_ref, lt_ref):
    tiles = B // S8
    for b in range(tiles):
        rows = pl.ds(b * S8, S8)
        d = d_ref[rows, :]
        m = m_ref[rows, :]
        cols = [rep(d[:, b * S8 + k : b * S8 + k + 1]) for k in range(S8)]
        s = {}
        for i in range(S8):
            for k in range(i, S8):
                s[i, k] = rep(cols[k][i : i + 1, :])
        rd = [rep(d[j : j + 1, :]) for j in range(S8)]
        rm = [rep(m[j : j + 1, :]) for j in range(S8)]
        u, qd, qm, scale = {}, [], [], []
        for j in range(S8):
            inv = 1.0 / s[j, j]
            scale.append(lax.rsqrt(s[j, j]))
            for k in range(j + 1, S8):
                u[j, k] = s[j, k] * inv
            for i in range(j + 1, S8):
                for k in range(i, S8):
                    s[i, k] = s[i, k] - s[j, i] * u[j, k]
            qd.append(rd[j] * inv)
            qm.append(rm[j] * inv)
            for k in range(j + 1, S8):
                rd[k] = rd[k] - s[j, k] * qd[j]
                rm[k] = rm[k] - s[j, k] * qm[j]
        for t in range(b + 1, tiles):
            at = pl.ds(t * S8, S8)
            dt = d_ref[at, :]
            mt = m_ref[at, :]
            c = [rep(dt[:, b * S8 + k : b * S8 + k + 1]) for k in range(S8)]
            for j in range(S8):
                for k in range(j + 1, S8):
                    c[k] = c[k] - c[j] * u[j, k]
            for j in range(S8):
                dt = dt - c[j] * qd[j]
                mt = mt - c[j] * qm[j]
            d_ref[at, :] = dt
            m_ref[at, :] = mt
        sub = lax.broadcasted_iota(jnp.int32, (S8, B), 0)
        od, om = rd[0] * scale[0], rm[0] * scale[0]
        for j in range(1, S8):
            od = jnp.where(sub == j, rd[j] * scale[j], od)
            om = jnp.where(sub == j, rm[j] * scale[j], om)
        lt_ref[rows, :] = od
        m_ref[rows, :] = om

def dot(a, b, dims=((1,), (0,))):
    return lax.dot_general(a, b, (dims, ((), ())), precision=HI, preferred_element_type=jnp.float32)

BLOCKS = tuple((i, j) for i in range(4) for j in range(i + 1))
N = 4 * B


def eliminate(first, last, l_ref, inv_ref, s_ref, d_ref, m_ref, lt_ref):
    r128 = lax.broadcasted_iota(jnp.int32, (B, B), 0)
    c128 = lax.broadcasted_iota(jnp.int32, (B, B), 1)
    eye = jnp.where(r128 == c128, 1.0, 0.0).astype(jnp.float32)
    for k in range(first, last):
        lo, hi = k * B, (k + 1) * B
        d_ref[...] = s_ref[lo:hi, lo:hi]
        m_ref[...] = eye
        factor_tile(d_ref, m_ref, lt_ref)
        inv = m_ref[...]
        l_ref[lo:hi, lo:hi] = jnp.where(r128 >= c128, lt_ref[...].T, 0.0)
        inv_ref[lo:hi, lo:hi] = inv
        if k:
            inv_ref[lo:hi, :lo] = dot(inv, inv_ref[lo:hi, :lo])
        if hi < N:
            below = dot(s_ref[hi:, lo:hi], inv, ((1,), (1,)))
            l_ref[hi:, lo:hi] = below
            for i in range(k + 1, N // B):
                a, z = i * B, (i + 1) * B
                mine = below[a - hi : z - hi]
                s_ref[a:z, hi:z] -= dot(mine, below[: z - hi], ((1,), (1,)))
                inv_ref[a:z, :hi] -= dot(mine, inv_ref[lo:hi, :hi])


def first_kernel(g_ref, after_ref, s_ref, l_ref, inv_ref, d_ref, m_ref, lt_ref):
    del after_ref
    s_ref[...] = jnp.zeros((N, N), jnp.float32)
    for at, (i, j) in enumerate(BLOCKS):
        s_ref[i * B : (i + 1) * B, j * B : (j + 1) * B] = g_ref[:, at].reshape(B, B)
    inv_ref[...] = jnp.zeros((N, N), jnp.float32)
    l_ref[...] = jnp.zeros((N, N), jnp.float32)
    eliminate(0, 2, l_ref, inv_ref, s_ref, d_ref, m_ref, lt_ref)


def second_kernel(s_in, l_in, inv_in, after_ref, s_ref, l_ref, inv_ref, d_ref, m_ref, lt_ref):
    del s_in, l_in, inv_in, after_ref
    eliminate(2, 4, l_ref, inv_ref, s_ref, d_ref, m_ref, lt_ref)


def whole():
    return pl.BlockSpec(memory_space=pltpu.VMEM)


def anywhere():
    return pl.BlockSpec(memory_space=pl.ANY)


PARAMS = pltpu.CompilerParams(vmem_limit_bytes=40 * 2**20)
SQUARE = jax.ShapeDtypeStruct((N, N), jnp.float32)


def first_half(gathered, after):
    return pl.pallas_call(
        first_kernel,
        out_shape=(SQUARE,) * 3,
        in_specs=[whole(), anywhere()],
        out_specs=(whole(),) * 3,
        scratch_shapes=[pltpu.VMEM((B, B), jnp.float32)] * 3,
        compiler_params=PARAMS,
    )(gathered, after)


def second_half(s, lower, inv, after):
    return pl.pallas_call(
        second_kernel,
        out_shape=(SQUARE,) * 3,
        in_specs=[whole()] * 3 + [anywhere()],
        out_specs=(whole(),) * 3,
        input_output_aliases={0: 0, 1: 1, 2: 2},
        scratch_shapes=[pltpu.VMEM((B, B), jnp.float32)] * 3,
        compiler_params=PARAMS,
    )(s, lower, inv, after)


def final_kernel(x_ref, own_ref, other_ref, top_ref, l_ref, inv_ref, panel_ref, out_ref, u_ref, f_ref):
    row, col = lax.axis_index("row"), lax.axis_index("col")
    inv = inv_ref[...]
    top = jnp.concatenate([top_ref[:, 0, i].reshape(B, -1) for i in range(4)], axis=0)
    u_ref[...] = dot(inv, top)
    even = lax.rem(col, 2) == 0
    half = 2 * B

    def factor(left_ref, right_ref):
        f_ref[:, :half] = dot(left_ref[...], inv[:half, :half], ((1,), (1,)))
        f_ref[:, half:] = dot(left_ref[...], inv[half:, :half], ((1,), (1,))) + dot(
            right_ref[...], inv[half:, half:], ((1,), (1,))
        )

    @pl.when(jnp.logical_and(row > 0, even))
    def _():
        factor(own_ref, other_ref)

    @pl.when(jnp.logical_and(row > 0, jnp.logical_not(even)))
    def _():
        factor(other_ref, own_ref)

    @pl.when(row == 0)
    def _():
        f_ref[...] = l_ref[...]

    panel_ref[...] = f_ref[pl.ds(pl.multiple_of(col * 16, 16), 16), :]
    live = jnp.logical_and(row > 0, col > 1)

    @pl.when(live)
    def _():
        out_ref[...] = x_ref[...] - dot(f_ref[...], u_ref[...])

    @pl.when(jnp.logical_not(live))
    def _():
        out_ref[...] = jnp.zeros_like(out_ref)


def final(x, own, other, top, lower, inv):
    return pl.pallas_call(
        final_kernel,
        out_shape=(
            jax.ShapeDtypeStruct((16, 512), jnp.float32),
            jax.ShapeDtypeStruct((512, 256), jnp.float32),
        ),
        in_specs=[whole()] * 6,
        out_specs=(whole(), whole()),
        scratch_shapes=[pltpu.VMEM((512, 256), jnp.float32), pltpu.VMEM((512, 512), jnp.float32)],
        compiler_params=PARAMS,
    )(x, own, other, top, lower, inv)


def either(value, options):
    found = value == options[0]
    for option in options[1:]:
        found = jnp.logical_or(found, value == option)
    return found


def merge_kernel(takes, have_ref, got_ref, after_ref, out_ref):
    del after_ref
    col = lax.axis_index("col")
    take = takes(col // 8, lax.rem(col, 8))

    @pl.when(take)
    def _():
        out_ref[...] = got_ref[...]

    @pl.when(jnp.logical_not(take))
    def _():
        out_ref[...] = have_ref[...]


def merge(takes, have, got, after):
    return pl.pallas_call(
        functools.partial(merge_kernel, takes),
        out_shape=jax.ShapeDtypeStruct(have.shape, have.dtype),
        in_specs=[whole(), whole(), anywhere()],
        out_specs=whole(),
        compiler_params=PARAMS,
    )(have, got, after)


def pack_kernel(piece_ref, swapped_ref, out_ref):
    col = lax.axis_index("col")

    def put(left_ref, right_ref):
        for at, (i, j) in enumerate(BLOCKS):
            side_ref = left_ref if j < 2 else right_ref
            out_ref[at] = side_ref[i, :, (j % 2) * B : (j % 2 + 1) * B]

    @pl.when(col == 0)
    def _():
        put(piece_ref, swapped_ref)

    @pl.when(col == 1)
    def _():
        put(swapped_ref, piece_ref)

    @pl.when(col > 1)
    def _():
        out_ref[...] = jnp.zeros_like(out_ref)


def pack(piece, swapped):
    return pl.pallas_call(
        pack_kernel,
        out_shape=jax.ShapeDtypeStruct((len(BLOCKS), 8, B), jnp.float32),
        in_specs=[whole()] * 2,
        out_specs=whole(),
        compiler_params=PARAMS,
    )(piece, swapped)


def on_device(x):
    planes = range(0, 32, 8)

    def send(v, pairs):
        return lax.ppermute(v, "col", pairs)

    got = send(x, [(0, 16), (1, 17)])

    split = x.reshape(4, 16, 8, 256).transpose(1, 0, 2, 3)
    turned = lax.all_to_all(split, "row", 0, 0)
    piece = turned[0]
    top = lax.all_gather(turned[:2], "row")
    half = merge(lambda z, xi: z != 0, x, got, piece)
    got = send(half, [(0, 8), (1, 9), (16, 24), (17, 25)])

    packed = pack(piece, send(piece, [(0, 1), (1, 0)]))
    packed += sum(send(packed, [(0, 8 * q), (1, 8 * q + 1)]) for q in range(1, 4))
    half = merge(lambda z, xi: lax.rem(z, 2) == 1, half, got, packed)
    got = send(half, [(p + i, p + j) for p in planes for i, j in ((0, 6), (1, 3))])
    packed += sum(send(packed, [(p + i, p + i + s) for p in planes for i in (0, 1)]) for s in (2, 4, 6))
    gathered = lax.all_gather(packed, "row")

    half = merge(lambda z, xi: either(xi, (3, 6)), half, got, gathered)
    got = send(half, [(p + i, p + j) for p in planes for i, j in ((0, 2), (6, 4), (1, 7), (3, 5))])
    state = first_half(gathered, half)
    half = merge(lambda z, xi: either(xi, (2, 4, 5, 7)), half, got, state[0])
    other = send(half, [(i, i ^ 1) for i in range(32)])
    _, lower, inv = second_half(*state, half)
    return final(x, half, other, top, lower, inv)


def solution(mesh):
    return jax.shard_map(
        on_device,
        mesh=mesh,
        in_specs=(P("row", "col"),),
        out_specs=(P(("row", "col"), None), P("row", "col")),
        check_vma=False,
    )
```

```python
import functools

import jax, jax.numpy as jnp
from jax import lax
from jax.experimental import pallas as pl
from jax.experimental.pallas import tpu as pltpu
from jax.sharding import PartitionSpec as P

HI = lax.Precision.HIGHEST
B = 128
S8 = 8

def rep(x):
    return jnp.broadcast_to(x, (S8, B))

def factor_tile(d_ref, m_ref, lt_ref):
    tiles = B // S8
    for b in range(tiles):
        rows = pl.ds(b * S8, S8)
        d = d_ref[rows, :]
        m = m_ref[rows, :]
        cols = [rep(d[:, b * S8 + k : b * S8 + k + 1]) for k in range(S8)]
        s = {}
        for i in range(S8):
            for k in range(i, S8):
                s[i, k] = rep(cols[k][i : i + 1, :])
        rd = [rep(d[j : j + 1, :]) for j in range(S8)]
        rm = [rep(m[j : j + 1, :]) for j in range(S8)]
        u, qd, qm, scale = {}, [], [], []
        for j in range(S8):
            inv = 1.0 / s[j, j]
            scale.append(lax.rsqrt(s[j, j]))
            for k in range(j + 1, S8):
                u[j, k] = s[j, k] * inv
            for i in range(j + 1, S8):
                for k in range(i, S8):
                    s[i, k] = s[i, k] - s[j, i] * u[j, k]
            qd.append(rd[j] * inv)
            qm.append(rm[j] * inv)
            for k in range(j + 1, S8):
                rd[k] = rd[k] - s[j, k] * qd[j]
                rm[k] = rm[k] - s[j, k] * qm[j]
        for t in range(b + 1, tiles):
            at = pl.ds(t * S8, S8)
            dt = d_ref[at, :]
            mt = m_ref[at, :]
            c = [rep(dt[:, b * S8 + k : b * S8 + k + 1]) for k in range(S8)]
            for j in range(S8):
                for k in range(j + 1, S8):
                    c[k] = c[k] - c[j] * u[j, k]
            for j in range(S8):
                dt = dt - c[j] * qd[j]
                mt = mt - c[j] * qm[j]
            d_ref[at, :] = dt
            m_ref[at, :] = mt
        sub = lax.broadcasted_iota(jnp.int32, (S8, B), 0)
        od, om = rd[0] * scale[0], rm[0] * scale[0]
        for j in range(1, S8):
            od = jnp.where(sub == j, rd[j] * scale[j], od)
            om = jnp.where(sub == j, rm[j] * scale[j], om)
        lt_ref[rows, :] = od
        m_ref[rows, :] = om

def dot(a, b, dims=((1,), (0,))):
    return lax.dot_general(a, b, (dims, ((), ())), precision=HI, preferred_element_type=jnp.float32)

N = 4 * B
LEFT = ((0, 0), (1, 0), (1, 1), (2, 0), (3, 0))
RIGHT = ((2, 2), (3, 2), (3, 3), (1, 2), (1, 3))


def eliminate(first, last, l_ref, inv_ref, s_ref, d_ref, m_ref, lt_ref):
    r128 = lax.broadcasted_iota(jnp.int32, (B, B), 0)
    c128 = lax.broadcasted_iota(jnp.int32, (B, B), 1)
    eye = jnp.where(r128 == c128, 1.0, 0.0).astype(jnp.float32)
    for k in range(first, last):
        lo, hi = k * B, (k + 1) * B
        d_ref[...] = s_ref[lo:hi, lo:hi]
        m_ref[...] = eye
        factor_tile(d_ref, m_ref, lt_ref)
        inv = m_ref[...]
        l_ref[lo:hi, lo:hi] = jnp.where(r128 >= c128, lt_ref[...].T, 0.0)
        inv_ref[lo:hi, lo:hi] = inv
        if k:
            inv_ref[lo:hi, :lo] = dot(inv, inv_ref[lo:hi, :lo])
        if hi < N:
            below = dot(s_ref[hi:, lo:hi], inv, ((1,), (1,)))
            l_ref[hi:, lo:hi] = below
            for i in range(k + 1, N // B):
                a, z = i * B, (i + 1) * B
                mine = below[a - hi : z - hi]
                s_ref[a:z, hi:z] -= dot(mine, below[: z - hi], ((1,), (1,)))
                inv_ref[a:z, :hi] -= dot(mine, inv_ref[lo:hi, :hi])


def first_kernel(g_ref, after_ref, s_ref, l_ref, inv_ref, d_ref, m_ref, lt_ref):
    del after_ref
    s_ref[...] = jnp.zeros((N, N), jnp.float32)
    for at, (i, j) in enumerate(LEFT + RIGHT):
        for r in range(16):
            p = (r % 2) * 8 + r // 2
            s_ref[i * B + p * 8 : i * B + p * 8 + 8, j * B : (j + 1) * B] = g_ref[r, at]
    for i, j in RIGHT[3:]:
        s_ref[j * B : (j + 1) * B, i * B : (i + 1) * B] = s_ref[i * B : (i + 1) * B, j * B : (j + 1) * B].T
    inv_ref[...] = jnp.zeros((N, N), jnp.float32)
    l_ref[...] = jnp.zeros((N, N), jnp.float32)
    eliminate(0, 3, l_ref, inv_ref, s_ref, d_ref, m_ref, lt_ref)


def second_kernel(s_in, l_in, inv_in, after_ref, s_ref, l_ref, inv_ref, d_ref, m_ref, lt_ref):
    del s_in, l_in, inv_in, after_ref
    eliminate(3, 4, l_ref, inv_ref, s_ref, d_ref, m_ref, lt_ref)


def whole():
    return pl.BlockSpec(memory_space=pltpu.VMEM)


def anywhere():
    return pl.BlockSpec(memory_space=pl.ANY)


PARAMS = pltpu.CompilerParams(vmem_limit_bytes=40 * 2**20)
SQUARE = jax.ShapeDtypeStruct((N, N), jnp.float32)


def first_half(gathered, after):
    return pl.pallas_call(
        first_kernel,
        out_shape=(SQUARE,) * 3,
        in_specs=[whole(), anywhere()],
        out_specs=(whole(),) * 3,
        scratch_shapes=[pltpu.VMEM((B, B), jnp.float32)] * 3,
        compiler_params=PARAMS,
    )(gathered, after)


def second_half(s, lower, inv, after):
    return pl.pallas_call(
        second_kernel,
        out_shape=(SQUARE,) * 3,
        in_specs=[whole()] * 3 + [anywhere()],
        out_specs=(whole(),) * 3,
        input_output_aliases={0: 0, 1: 1, 2: 2},
        scratch_shapes=[pltpu.VMEM((B, B), jnp.float32)] * 3,
        compiler_params=PARAMS,
    )(s, lower, inv, after)


def final_kernel(x_ref, mine_ref, f1_ref, f2_ref, f3_ref, top_ref, far_ref, l_ref, inv_ref, panel_ref, out_ref, u_ref, f_ref):
    row, col = lax.axis_index("row"), lax.axis_index("col")
    inv = inv_ref[...]

    @pl.when(lax.rem(row, 2) == 0)
    def _():
        u_ref[...] = dot(inv, top_ref[...])

    @pl.when(lax.rem(row, 2) == 1)
    def _():
        u_ref[...] = dot(inv, far_ref[...])

    @pl.when(row == 0)
    def _():
        f_ref[...] = l_ref[...]

    @pl.when(row > 0)
    def _():
        for s, ref in enumerate((mine_ref, f1_ref, f2_ref, f3_ref)):
            at = pl.multiple_of(lax.rem(col // 8 + 4 - s, 4) * B, B)
            f_ref[pl.ds(at, B), :] = dot(ref[...], inv, ((1,), (1,)))

    panel_ref[...] = f_ref[pl.ds(pl.multiple_of(col * 16, 16), 16), :]
    live = jnp.logical_and(row > 0, col > 1)

    @pl.when(live)
    def _():
        out_ref[...] = x_ref[...] - dot(f_ref[...], u_ref[...])

    @pl.when(jnp.logical_not(live))
    def _():
        out_ref[...] = jnp.zeros_like(out_ref)


def final(x, mine, far, top, down, lower, inv):
    return pl.pallas_call(
        final_kernel,
        out_shape=(
            jax.ShapeDtypeStruct((16, 512), jnp.float32),
            jax.ShapeDtypeStruct((512, 256), jnp.float32),
        ),
        in_specs=[whole()] * 9,
        out_specs=(whole(), whole()),
        scratch_shapes=[pltpu.VMEM((512, 256), jnp.float32), pltpu.VMEM((512, 512), jnp.float32)],
        compiler_params=PARAMS,
    )(x, mine, *far, top, down, lower, inv)


def place():
    row, col = lax.axis_index("row"), lax.axis_index("col")
    return row // 2, lax.rem(row, 2), col // 8, lax.rem(col, 8)


def either(value, options):
    found = value == options[0]
    for option in options[1:]:
        found = jnp.logical_or(found, value == option)
    return found


def choose(out_ref, take, yes_ref, no_ref):
    @pl.when(take)
    def _():
        out_ref[...] = yes_ref[...]

    @pl.when(jnp.logical_not(take))
    def _():
        out_ref[...] = no_ref[...]


def like(*values):
    return tuple(jax.ShapeDtypeStruct(v.shape, v.dtype) for v in values)


def local(kernel, values, outs, aliases={}):
    return pl.pallas_call(
        kernel,
        out_shape=outs,
        in_specs=[whole()] * len(values),
        out_specs=(whole(),) * len(outs),
        input_output_aliases=aliases,
        compiler_params=PARAMS,
    )(*values)


def spread_kernel(x_ref, f1_ref, f2_ref, f3_ref, cur_ref, half_ref, piece_ref):
    y, core, z, xi = place()
    for q, ref in enumerate((None, f1_ref, f2_ref, f3_ref)):

        @pl.when(z == q)
        def _(q=q, ref=ref):
            half_ref[...] = x_ref[:B] if q == 0 else ref[...]

    holds = jnp.logical_and(z == 0, xi < 2)

    @pl.when(holds)
    def _():
        piece_ref[...] = cur_ref[0]

    @pl.when(jnp.logical_not(holds))
    def _():
        piece_ref[...] = jnp.zeros_like(piece_ref)


def pair_kernel(own_ref, other_ref, half_ref, far_ref, x_ref, down_ref, both_ref, half_out, top_ref):
    y, core, z, xi = place()
    even = lax.rem(xi, 2) == 0

    @pl.when(z > 0)
    def _():
        both_ref[...] = jnp.zeros_like(both_ref)

    @pl.when(jnp.logical_and(z == 0, even))
    def _():
        both_ref[:5] = own_ref[...]
        both_ref[5:] = other_ref[...]

    @pl.when(jnp.logical_and(z == 0, jnp.logical_not(even)))
    def _():
        both_ref[:5] = other_ref[...]
        both_ref[5:] = own_ref[...]

    choose(half_out, xi >= 4, far_ref, half_ref)
    choose(top_ref, y >= 4, down_ref, x_ref)


def sum_kernel(b0_ref, b1_ref, b2_ref, b3_ref, half_ref, far_ref, both_ref, half_out):
    y, core, z, xi = place()
    both_ref[...] = (b0_ref[...] + b1_ref[...]) + (b2_ref[...] + b3_ref[...])
    choose(half_out, either(lax.rem(xi, 4), (2, 3)), far_ref, half_ref)


def join_kernel(g_in, half_ref, far_ref, top_ref, down_ref, g_ref, mine_ref, top_out):
    del g_in, g_ref
    y, core, z, xi = place()
    even = lax.rem(xi, 2) == 0
    left, right = mine_ref.at[:, : 2 * B], mine_ref.at[:, 2 * B :]
    choose(left, even, half_ref, far_ref)
    choose(right, even, far_ref, half_ref)
    choose(top_out, lax.rem(y // 2, 2) == 1, down_ref, top_ref)


def last_kernel(s_in, top_ref, down_ref, f1_ref, f2_ref, f3_ref, s_ref, top_out):
    del s_in, s_ref, f1_ref, f2_ref, f3_ref
    y, core, z, xi = place()
    choose(top_out, lax.rem(y, 2) == 1, down_ref, top_ref)


def pack_kernel(x_ref, out_ref):
    def put(blocks):
        for at, (i, j) in enumerate(blocks):
            j = j % 2
            for p in range(16):
                out_ref[p, at] = x_ref[i * B + p * 8 : i * B + p * 8 + 8, j * B : (j + 1) * B]

    @pl.when(lax.axis_index("col") == 0)
    def _():
        put(LEFT)

    @pl.when(lax.axis_index("col") > 0)
    def _():
        put(RIGHT)


def pack(x):
    return pl.pallas_call(
        pack_kernel,
        out_shape=jax.ShapeDtypeStruct((16, 5, 8, B), jnp.float32),
        in_specs=[whole()],
        out_specs=whole(),
        compiler_params=PARAMS,
    )(x)


def on_device(x):
    row = lax.axis_index("row")
    planes = range(0, 32, 8)

    def along(v, pairs):
        return lax.ppermute(v, "col", pairs)

    def across(v, pairs):
        return lax.ppermute(v, "row", pairs)

    far = [along(x[q * B : (q + 1) * B], [(0, 8 * q), (1, 8 * q + 1)]) for q in (1, 2, 3)]
    down = across(x, [(0, 8)])

    cur = pack(x)
    got = across(cur[8:], [(0, 1)])
    cur = jnp.where(row % 2 == 1, got, cur[:8])
    for step in (4, 2, 1):
        pairs = [(2 * y + k, 2 * (y + step) + k) for y in range(0, 8, 2 * step) for k in (0, 1)]
        got = across(cur[step:], pairs)
        cur = jnp.where((row // 2) // step % 2 == 1, got, cur[:step])

    quarter = jax.ShapeDtypeStruct((B, 2 * B), jnp.float32)
    some = jax.ShapeDtypeStruct((5, 8, B), jnp.float32)
    full = jax.ShapeDtypeStruct((10, 8, B), jnp.float32)
    half, piece = local(spread_kernel, (x, *far, cur), (quarter, some))
    far = along(half, [(p + i, p + i + 4) for p in planes for i in (0, 1)])
    piece += sum(along(piece, [(0, s), (1, 1 + s)]) for s in (2, 4, 6))
    swapped = along(piece, [(i, i ^ 1) for i in range(8)])
    both, half, top = local(
        pair_kernel, (piece, swapped, half, far, x, down), (full, quarter) + like(x)
    )
    far = along(half, [(p + i, p + i + 2) for p in planes for i in (0, 1, 4, 5)])
    down = across(top, [(0, 4), (8, 12)])
    parts = [along(both, [(i, 8 * q + i) for i in range(8)]) for q in (1, 2, 3)]
    both, half = local(sum_kernel, (both, *parts, half, far), (full, quarter))
    other = along(half, [(i, i ^ 1) for i in range(32)])
    gathered = lax.all_gather(both, "row")

    wide = jax.ShapeDtypeStruct((B, 4 * B), jnp.float32)
    gathered, mine, top = local(
        join_kernel, (gathered, half, other, top, down), like(gathered) + (wide,) + like(top), {0: 0}
    )
    far = [along(mine, [(i, (i + 8 * s) % 32) for i in range(32)]) for s in (1, 2, 3)]
    down = across(top, [(4 * q, 4 * q + 2) for q in range(4)])
    s, lower, inv = first_half(gathered, mine)
    s, top = local(last_kernel, (s, top, down, *far), like(s, top), {0: 0})
    down = across(top, [(2 * q, 2 * q + 1) for q in range(8)])
    _, lower, inv = second_half(s, lower, inv, top)
    return final(x, mine, far, top, down, lower, inv)


def solution(mesh):
    return jax.shard_map(
        on_device,
        mesh=mesh,
        in_specs=(P("row", "col"),),
        out_specs=(P(("row", "col"), None), P("row", "col")),
        check_vma=False,
    )
```

```python
import functools

import jax, jax.numpy as jnp
from jax import lax
from jax.experimental import pallas as pl
from jax.experimental.pallas import tpu as pltpu
from jax.sharding import PartitionSpec as P

HI = lax.Precision.HIGHEST
B = 128
S8 = 8

def rep(x):
    return jnp.broadcast_to(x, (S8, B))

def factor_tile(d_ref, m_ref, lt_ref):
    tiles = B // S8
    for b in range(tiles):
        rows = pl.ds(b * S8, S8)
        d = d_ref[rows, :]
        m = m_ref[rows, :]
        cols = [rep(d[:, b * S8 + k : b * S8 + k + 1]) for k in range(S8)]
        s = {}
        for i in range(S8):
            for k in range(i, S8):
                s[i, k] = rep(cols[k][i : i + 1, :])
        rd = [rep(d[j : j + 1, :]) for j in range(S8)]
        rm = [rep(m[j : j + 1, :]) for j in range(S8)]
        u, qd, qm, scale = {}, [], [], []
        for j in range(S8):
            inv = 1.0 / s[j, j]
            scale.append(lax.rsqrt(s[j, j]))
            for k in range(j + 1, S8):
                u[j, k] = s[j, k] * inv
            for i in range(j + 1, S8):
                for k in range(i, S8):
                    s[i, k] = s[i, k] - s[j, i] * u[j, k]
            qd.append(rd[j] * inv)
            qm.append(rm[j] * inv)
            for k in range(j + 1, S8):
                rd[k] = rd[k] - s[j, k] * qd[j]
                rm[k] = rm[k] - s[j, k] * qm[j]
        for t in range(b + 1, tiles):
            at = pl.ds(t * S8, S8)
            dt = d_ref[at, :]
            mt = m_ref[at, :]
            c = [rep(dt[:, b * S8 + k : b * S8 + k + 1]) for k in range(S8)]
            for j in range(S8):
                for k in range(j + 1, S8):
                    c[k] = c[k] - c[j] * u[j, k]
            for j in range(S8):
                dt = dt - c[j] * qd[j]
                mt = mt - c[j] * qm[j]
            d_ref[at, :] = dt
            m_ref[at, :] = mt
        sub = lax.broadcasted_iota(jnp.int32, (S8, B), 0)
        od, om = rd[0] * scale[0], rm[0] * scale[0]
        for j in range(1, S8):
            od = jnp.where(sub == j, rd[j] * scale[j], od)
            om = jnp.where(sub == j, rm[j] * scale[j], om)
        lt_ref[rows, :] = od
        m_ref[rows, :] = om

def dot(a, b, dims=((1,), (0,))):
    return lax.dot_general(a, b, (dims, ((), ())), precision=HI, preferred_element_type=jnp.float32)

N = 4 * B
LEFT = ((0, 0), (1, 0), (1, 1), (2, 0), (3, 0))
RIGHT = ((2, 2), (3, 2), (3, 3), (1, 2), (1, 3))


def eliminate(first, last, l_ref, inv_ref, s_ref, d_ref, m_ref, lt_ref):
    r128 = lax.broadcasted_iota(jnp.int32, (B, B), 0)
    c128 = lax.broadcasted_iota(jnp.int32, (B, B), 1)
    eye = jnp.where(r128 == c128, 1.0, 0.0).astype(jnp.float32)
    for k in range(first, last):
        lo, hi = k * B, (k + 1) * B
        d_ref[...] = s_ref[lo:hi, lo:hi]
        m_ref[...] = eye
        factor_tile(d_ref, m_ref, lt_ref)
        inv = m_ref[...]
        l_ref[lo:hi, lo:hi] = jnp.where(r128 >= c128, lt_ref[...].T, 0.0)
        inv_ref[lo:hi, lo:hi] = inv
        if k:
            inv_ref[lo:hi, :lo] = dot(inv, inv_ref[lo:hi, :lo])
        if hi < N:
            below = dot(s_ref[hi:, lo:hi], inv, ((1,), (1,)))
            l_ref[hi:, lo:hi] = below
            for i in range(k + 1, N // B):
                a, z = i * B, (i + 1) * B
                mine = below[a - hi : z - hi]
                s_ref[a:z, hi:z] -= dot(mine, below[: z - hi], ((1,), (1,)))
                inv_ref[a:z, :hi] -= dot(mine, inv_ref[lo:hi, :hi])


def first_kernel(g_ref, after_ref, s_ref, l_ref, inv_ref, d_ref, m_ref, lt_ref):
    del after_ref
    s_ref[...] = jnp.zeros((N, N), jnp.float32)
    for at, (i, j) in enumerate(LEFT + RIGHT):
        for r in range(16):
            p = (r % 2) * 8 + r // 2
            s_ref[i * B + p * 8 : i * B + p * 8 + 8, j * B : (j + 1) * B] = g_ref[r, at]
    for i, j in RIGHT[3:]:
        s_ref[j * B : (j + 1) * B, i * B : (i + 1) * B] = s_ref[i * B : (i + 1) * B, j * B : (j + 1) * B].T
    inv_ref[...] = jnp.zeros((N, N), jnp.float32)
    l_ref[...] = jnp.zeros((N, N), jnp.float32)
    eliminate(0, 2, l_ref, inv_ref, s_ref, d_ref, m_ref, lt_ref)


def second_kernel(s_in, l_in, inv_in, after_ref, s_ref, l_ref, inv_ref, d_ref, m_ref, lt_ref):
    del s_in, l_in, inv_in, after_ref
    eliminate(2, 4, l_ref, inv_ref, s_ref, d_ref, m_ref, lt_ref)


def whole():
    return pl.BlockSpec(memory_space=pltpu.VMEM)


def anywhere():
    return pl.BlockSpec(memory_space=pl.ANY)


PARAMS = pltpu.CompilerParams(vmem_limit_bytes=40 * 2**20)
SQUARE = jax.ShapeDtypeStruct((N, N), jnp.float32)


def first_half(gathered, after):
    return pl.pallas_call(
        first_kernel,
        out_shape=(SQUARE,) * 3,
        in_specs=[whole(), anywhere()],
        out_specs=(whole(),) * 3,
        scratch_shapes=[pltpu.VMEM((B, B), jnp.float32)] * 3,
        compiler_params=PARAMS,
    )(gathered, after)


def second_half(s, lower, inv, after):
    return pl.pallas_call(
        second_kernel,
        out_shape=(SQUARE,) * 3,
        in_specs=[whole()] * 3 + [anywhere()],
        out_specs=(whole(),) * 3,
        input_output_aliases={0: 0, 1: 1, 2: 2},
        scratch_shapes=[pltpu.VMEM((B, B), jnp.float32)] * 3,
        compiler_params=PARAMS,
    )(s, lower, inv, after)


def final_kernel(x_ref, q0_ref, q1_ref, q2_ref, q3_ref, top_ref, far_ref, l_ref, inv_ref, panel_ref, out_ref, u_ref, f_ref):
    row, col = lax.axis_index("row"), lax.axis_index("col")
    inv = inv_ref[...]
    half = 2 * B

    def solve_top(ref):
        u_ref[:half] = dot(inv[:half, :half], ref[:half])
        u_ref[half:] = dot(inv[half:], ref[...])

    @pl.when(lax.rem(row, 2) == 0)
    def _():
        solve_top(top_ref)

    @pl.when(lax.rem(row, 2) == 1)
    def _():
        solve_top(far_ref)

    @pl.when(row == 0)
    def _():
        f_ref[...] = l_ref[...]

    for x in range(4):

        @pl.when(jnp.logical_and(row > 0, lax.rem(col, 4) == x))
        def _(x=x):
            held = {x: q0_ref, (x + 3) % 4: q1_ref, (x + 1) % 4: q2_ref, (x + 2) % 4: q3_ref}
            for lo, left, right in ((0, held[0], held[1]), (half, held[3], held[2])):
                f_ref[lo : lo + half, :half] = dot(left[...], inv[:half, :half], ((1,), (1,)))
                f_ref[lo : lo + half, half:] = dot(left[...], inv[half:, :half], ((1,), (1,))) + dot(
                    right[...], inv[half:, half:], ((1,), (1,))
                )

    panel_ref[...] = f_ref[pl.ds(pl.multiple_of(col * 16, 16), 16), :]
    live = jnp.logical_and(row > 0, col > 1)

    @pl.when(live)
    def _():
        out_ref[...] = x_ref[...] - lax.dot_general(
            f_ref[...],
            u_ref[...],
            (((1,), (0,)), ((), ())),
            precision=lax.Precision.HIGH,
            preferred_element_type=jnp.float32,
        )

    @pl.when(jnp.logical_not(live))
    def _():
        out_ref[...] = jnp.zeros_like(out_ref)


def final(*values):
    return pl.pallas_call(
        final_kernel,
        out_shape=(
            jax.ShapeDtypeStruct((16, 512), jnp.float32),
            jax.ShapeDtypeStruct((512, 256), jnp.float32),
        ),
        in_specs=[whole()] * 9,
        out_specs=(whole(), whole()),
        scratch_shapes=[pltpu.VMEM((512, 256), jnp.float32), pltpu.VMEM((512, 512), jnp.float32)],
        compiler_params=PARAMS,
    )(*values)


def place():
    row, col = lax.axis_index("row"), lax.axis_index("col")
    return row // 2, lax.rem(row, 2), col // 4, lax.rem(col, 4)


def choose(out_ref, take, yes_ref, no_ref):
    @pl.when(take)
    def _():
        out_ref[...] = yes_ref[...]

    @pl.when(jnp.logical_not(take))
    def _():
        out_ref[...] = no_ref[...]


def f32(*shape):
    return jax.ShapeDtypeStruct(shape, jnp.float32)


def local(kernel, values, outs, aliases={}):
    return pl.pallas_call(
        kernel,
        out_shape=outs,
        in_specs=[whole()] * len(values),
        out_specs=(whole(),) * len(outs),
        input_output_aliases=aliases,
        compiler_params=PARAMS,
    )(*values)


def pack_kernel(x_ref, low_ref, high_ref):
    def put(blocks):
        for at, (i, j) in enumerate(blocks):
            j = j % 2
            for p in range(16):
                part = low_ref if p < 8 else high_ref
                part[p % 8, at] = x_ref[i * B + p * 8 : i * B + p * 8 + 8, j * B : (j + 1) * B]

    @pl.when(lax.axis_index("col") == 0)
    def _():
        put(LEFT)

    @pl.when(lax.axis_index("col") > 0)
    def _():
        put(RIGHT)


def halve(take, got_ref, have_ref, low_ref, high_ref):
    n = low_ref.shape[0]
    choose(low_ref, take, got_ref.at[:n], have_ref.at[:n])
    choose(high_ref, take, got_ref.at[n:], have_ref.at[n:])


def core_kernel(have_ref, got_ref, low_ref, high_ref):
    halve(place()[1] == 1, got_ref, have_ref, low_ref, high_ref)


def y4_kernel(have_ref, got_ref, x_ref, far_ref, low_ref, high_ref, quarter_ref):
    y, core, z, xi = place()
    halve(y >= 4, got_ref, have_ref, low_ref, high_ref)
    choose(quarter_ref, xi >= 2, far_ref, x_ref.at[: 2 * B])


def y2_kernel(have_ref, got_ref, low_ref, high_ref):
    halve(lax.rem(place()[0] // 2, 2) == 1, got_ref, have_ref, low_ref, high_ref)


def y1_kernel(have_ref, got_ref, x_ref, quarter_ref, far_ref, piece_ref, top_ref, quarter_out):
    y, core, z, xi = place()
    choose(quarter_out, z >= 4, far_ref, quarter_ref)
    top_ref[...] = x_ref[...]
    holds = jnp.logical_and(z == 0, xi < 2)

    @pl.when(holds)
    def _():
        choose(piece_ref, lax.rem(y, 2) == 1, got_ref.at[0], have_ref.at[0])

    @pl.when(jnp.logical_not(holds))
    def _():
        piece_ref[...] = jnp.zeros_like(piece_ref)


def z_kernel(quarter_in, have_ref, got_ref, top_ref, down_ref, quarter_ref, piece_ref, top_out):
    del quarter_in, quarter_ref
    y, core, z, xi = place()
    choose(piece_ref, lax.rem(z, 2) == 1, got_ref, have_ref)
    choose(top_out, y >= 4, down_ref, top_ref)


def x_kernel(own_ref, o1_ref, o2_ref, o3_ref, quarter_ref, far_ref, top_ref, down_ref, both_ref, quarter_out, top_out):
    y, core, z, xi = place()
    sides = ((own_ref, o1_ref), (o1_ref, own_ref), (o2_ref, o3_ref), (o3_ref, o2_ref))
    for x, (left, right) in enumerate(sides):

        @pl.when(xi == x)
        def _(left=left, right=right):
            both_ref[:5] = left[...]
            both_ref[5:] = right[...]

    choose(quarter_out, lax.rem(z // 2, 2) == 1, far_ref, quarter_ref)
    choose(top_out, lax.rem(y // 2, 2) == 1, down_ref, top_ref)


def gate_kernel(g_in, top_in, quarter_ref, far_ref, g_ref, top_ref, quarter_out):
    del g_in, top_in, g_ref, top_ref
    choose(quarter_out, lax.rem(place()[2], 2) == 1, far_ref, quarter_ref)


def mid_kernel(s_in, q1_in, q2_in, top_ref, down_ref, s_ref, q1_ref, q2_ref, top_out):
    del s_in, q1_in, q2_in, s_ref, q1_ref, q2_ref
    choose(top_out, lax.rem(place()[0], 2) == 1, down_ref, top_ref)


def on_device(x):
    zs, xs, ys = range(8), range(4), range(8)

    def along(v, pairs):
        return lax.ppermute(v, "col", pairs)

    def across(v, pairs):
        return lax.ppermute(v, "row", pairs)

    def by_z(v, step):
        holders = range(0, 8, 2 * step)
        return along(v, [(4 * z + i, 4 * (z + step) + i) for z in holders for i in xs])

    def by_x(v, step):
        return along(v, [(4 * z + i, 4 * z + (i + step) % 4) for z in zs for i in xs])

    far = along(x[2 * B :], [(0, 3), (1, 2)])
    low, high = local(pack_kernel, (x,), (f32(8, 5, 8, B),) * 2)
    got = across(high, [(0, 1)])
    low, high = local(core_kernel, (low, got), (f32(4, 5, 8, B),) * 2)
    got = across(high, [(0, 8), (1, 9)])
    quarter = f32(2 * B, 2 * B)
    low, high, part = local(y4_kernel, (low, got, x, far), (f32(2, 5, 8, B),) * 2 + (quarter,))
    far = by_z(part, 4)
    got = across(high, [(0, 4), (1, 5), (8, 12), (9, 13)])
    low, high = local(y2_kernel, (low, got), (f32(1, 5, 8, B),) * 2)
    got = across(high, [(4 * q + k, 4 * q + k + 2) for q in range(4) for k in (0, 1)])
    piece, top, part = local(y1_kernel, (low, got, x, part, far), (f32(5, 8, B), f32(*x.shape), quarter))

    down = across(top, [(0, 8)])
    piece += sum(along(piece, [(0, 4 * z), (1, 4 * z + 1)]) for z in (4, 2, 6))
    got = along(piece, [(4 * z + i, 4 * z + 4 + i) for z in (0, 2, 4, 6) for i in (0, 1)])
    part, piece, top = local(
        z_kernel, (part, piece, got, top, down), (quarter, f32(5, 8, B), f32(*x.shape)), {0: 0}
    )
    others = [
        along(piece, [(4 * z + i, 4 * z + j) for z in zs for i, j in pairs])
        for pairs in (((0, 1), (1, 0)), ((0, 2), (1, 3)), ((0, 3), (1, 2)))
    ]
    far = by_z(part, 2)
    down = across(top, [(0, 4), (8, 12)])
    both, part, top = local(
        x_kernel, (piece, *others, part, far, top, down), (f32(10, 8, B), quarter, f32(*x.shape))
    )
    far = by_z(part, 1)
    gathered = lax.all_gather(both, "row")
    gathered, top, part = local(
        gate_kernel, (gathered, top, part, far), (f32(16, 10, 8, B), f32(*x.shape), quarter), {0: 0, 1: 1}
    )
    down = across(top, [(4 * q, 4 * q + 2) for q in range(4)])
    near, next_ = by_x(part, 1), by_x(part, 3)
    s, lower, inv = first_half(gathered, part)
    s, near, next_, top = local(
        mid_kernel, (s, near, next_, top, down), (SQUARE, quarter, quarter, f32(*x.shape)), {0: 0, 1: 1, 2: 2}
    )
    down = across(top, [(2 * y, 2 * y + 1) for y in ys])
    opposite = by_x(near, 1)
    _, lower, inv = second_half(s, lower, inv, top)
    return final(x, part, near, next_, opposite, top, down, lower, inv)


def solution(mesh):
    return jax.shard_map(
        on_device,
        mesh=mesh,
        in_specs=(P("row", "col"),),
        out_specs=(P(("row", "col"), None), P("row", "col")),
        check_vma=False,
    )
```

```python
import functools

import jax, jax.numpy as jnp
from jax import lax
from jax.experimental import pallas as pl
from jax.experimental.pallas import tpu as pltpu
from jax.sharding import PartitionSpec as P

HI = lax.Precision.HIGHEST
B = 128
S8 = 8

def rep(x):
    return jnp.broadcast_to(x, (S8, B))

def factor_tile(d_ref, m_ref, lt_ref):
    tiles = B // S8
    for b in range(tiles):
        rows = pl.ds(b * S8, S8)
        d = d_ref[rows, :]
        m = m_ref[rows, :]
        cols = [rep(d[:, b * S8 + k : b * S8 + k + 1]) for k in range(S8)]
        s = {}
        for i in range(S8):
            for k in range(i, S8):
                s[i, k] = rep(cols[k][i : i + 1, :])
        rd = [rep(d[j : j + 1, :]) for j in range(S8)]
        rm = [rep(m[j : j + 1, :]) for j in range(S8)]
        u, qd, qm, scale = {}, [], [], []
        for j in range(S8):
            inv = 1.0 / s[j, j]
            scale.append(lax.rsqrt(s[j, j]))
            for k in range(j + 1, S8):
                u[j, k] = s[j, k] * inv
            for i in range(j + 1, S8):
                for k in range(i, S8):
                    s[i, k] = s[i, k] - s[j, i] * u[j, k]
            qd.append(rd[j] * inv)
            qm.append(rm[j] * inv)
            for k in range(j + 1, S8):
                rd[k] = rd[k] - s[j, k] * qd[j]
                rm[k] = rm[k] - s[j, k] * qm[j]
        for t in range(b + 1, tiles):
            at = pl.ds(t * S8, S8)
            dt = d_ref[at, :]
            mt = m_ref[at, :]
            c = [rep(dt[:, b * S8 + k : b * S8 + k + 1]) for k in range(S8)]
            for j in range(S8):
                for k in range(j + 1, S8):
                    c[k] = c[k] - c[j] * u[j, k]
            for j in range(S8):
                dt = dt - c[j] * qd[j]
                mt = mt - c[j] * qm[j]
            d_ref[at, :] = dt
            m_ref[at, :] = mt
        sub = lax.broadcasted_iota(jnp.int32, (S8, B), 0)
        od, om = rd[0] * scale[0], rm[0] * scale[0]
        for j in range(1, S8):
            od = jnp.where(sub == j, rd[j] * scale[j], od)
            om = jnp.where(sub == j, rm[j] * scale[j], om)
        lt_ref[rows, :] = od
        m_ref[rows, :] = om

def dot(a, b, dims=((1,), (0,))):
    return lax.dot_general(a, b, (dims, ((), ())), precision=HI, preferred_element_type=jnp.float32)

N = 4 * B
LEFT = ((0, 0), (1, 0), (1, 1), (2, 0), (3, 0))
RIGHT = ((2, 2), (3, 2), (3, 3), (1, 2), (1, 3))


def eliminate(first, last, l_ref, inv_ref, s_ref, d_ref, m_ref, lt_ref):
    r128 = lax.broadcasted_iota(jnp.int32, (B, B), 0)
    c128 = lax.broadcasted_iota(jnp.int32, (B, B), 1)
    eye = jnp.where(r128 == c128, 1.0, 0.0).astype(jnp.float32)
    for k in range(first, last):
        lo, hi = k * B, (k + 1) * B
        d_ref[...] = s_ref[lo:hi, lo:hi]
        m_ref[...] = eye
        factor_tile(d_ref, m_ref, lt_ref)
        inv = m_ref[...]
        l_ref[lo:hi, lo:hi] = jnp.where(r128 >= c128, lt_ref[...].T, 0.0)
        inv_ref[lo:hi, lo:hi] = inv
        if k:
            inv_ref[lo:hi, :lo] = dot(inv, inv_ref[lo:hi, :lo])
        if hi < N:
            below = dot(s_ref[hi:, lo:hi], inv, ((1,), (1,)))
            l_ref[hi:, lo:hi] = below
            for i in range(k + 1, N // B):
                a, z = i * B, (i + 1) * B
                mine = below[a - hi : z - hi]
                s_ref[a:z, hi:z] -= dot(mine, below[: z - hi], ((1,), (1,)))
                inv_ref[a:z, :hi] -= dot(mine, inv_ref[lo:hi, :hi])


def first_kernel(g_ref, after_ref, s_ref, l_ref, inv_ref, d_ref, m_ref, lt_ref):
    del after_ref
    s_ref[...] = jnp.zeros((N, N), jnp.float32)
    for at, (i, j) in enumerate(LEFT + RIGHT):
        for r in range(16):
            p = (r % 2) * 8 + r // 2
            s_ref[i * B + p * 8 : i * B + p * 8 + 8, j * B : (j + 1) * B] = g_ref[r, at]
    for i, j in RIGHT[3:]:
        s_ref[j * B : (j + 1) * B, i * B : (i + 1) * B] = s_ref[i * B : (i + 1) * B, j * B : (j + 1) * B].T
    inv_ref[...] = jnp.zeros((N, N), jnp.float32)
    l_ref[...] = jnp.zeros((N, N), jnp.float32)
    eliminate(0, 2, l_ref, inv_ref, s_ref, d_ref, m_ref, lt_ref)


def second_kernel(s_in, l_in, inv_in, after_ref, s_ref, l_ref, inv_ref, d_ref, m_ref, lt_ref):
    del s_in, l_in, inv_in, after_ref
    eliminate(2, 4, l_ref, inv_ref, s_ref, d_ref, m_ref, lt_ref)


def whole():
    return pl.BlockSpec(memory_space=pltpu.VMEM)


def anywhere():
    return pl.BlockSpec(memory_space=pl.ANY)


PARAMS = pltpu.CompilerParams(vmem_limit_bytes=40 * 2**20)
SQUARE = jax.ShapeDtypeStruct((N, N), jnp.float32)


def first_half(gathered, after):
    return pl.pallas_call(
        first_kernel,
        out_shape=(SQUARE,) * 3,
        in_specs=[whole(), anywhere()],
        out_specs=(whole(),) * 3,
        scratch_shapes=[pltpu.VMEM((B, B), jnp.float32)] * 3,
        compiler_params=PARAMS,
    )(gathered, after)


def second_half(s, lower, inv, after):
    return pl.pallas_call(
        second_kernel,
        out_shape=(SQUARE,) * 3,
        in_specs=[whole()] * 3 + [anywhere()],
        out_specs=(whole(),) * 3,
        input_output_aliases={0: 0, 1: 1, 2: 2},
        scratch_shapes=[pltpu.VMEM((B, B), jnp.float32)] * 3,
        compiler_params=PARAMS,
    )(s, lower, inv, after)


def final_kernel(x_ref, q0_ref, q1_ref, q2_ref, q3_ref, top_ref, far_ref, l_ref, inv_ref, panel_ref, out_ref, u_ref, f_ref):
    row, col = lax.axis_index("row"), lax.axis_index("col")
    inv = inv_ref[...]
    half = 2 * B

    def solve_top(ref):
        u_ref[:half] = dot(inv[:half, :half], ref[:half])
        u_ref[half:] = dot(inv[half:], ref[...])

    @pl.when(lax.rem(row, 2) == 0)
    def _():
        solve_top(top_ref)

    @pl.when(lax.rem(row, 2) == 1)
    def _():
        solve_top(far_ref)

    @pl.when(row == 0)
    def _():
        f_ref[...] = l_ref[...]

    for x in range(4):

        @pl.when(jnp.logical_and(row > 0, lax.rem(col, 4) == x))
        def _(x=x):
            held = {x: q0_ref, (x + 3) % 4: q1_ref, (x + 1) % 4: q2_ref, (x + 2) % 4: q3_ref}
            for lo, left, right in ((0, held[0], held[1]), (half, held[3], held[2])):
                f_ref[lo : lo + half, :half] = dot(left[...], inv[:half, :half], ((1,), (1,)))
                f_ref[lo : lo + half, half:] = dot(left[...], inv[half:, :half], ((1,), (1,))) + dot(
                    right[...], inv[half:, half:], ((1,), (1,))
                )

    panel_ref[...] = f_ref[pl.ds(pl.multiple_of(col * 16, 16), 16), :]
    live = jnp.logical_and(row > 0, col > 1)

    @pl.when(live)
    def _():
        out_ref[...] = x_ref[...] - lax.dot_general(
            f_ref[...],
            u_ref[...],
            (((1,), (0,)), ((), ())),
            precision=lax.Precision.HIGH,
            preferred_element_type=jnp.float32,
        )

    @pl.when(jnp.logical_not(live))
    def _():
        out_ref[...] = jnp.zeros_like(out_ref)


def final(*values):
    return pl.pallas_call(
        final_kernel,
        out_shape=(
            jax.ShapeDtypeStruct((16, 512), jnp.float32),
            jax.ShapeDtypeStruct((512, 256), jnp.float32),
        ),
        in_specs=[whole()] * 9,
        out_specs=(whole(), whole()),
        scratch_shapes=[pltpu.VMEM((512, 256), jnp.float32), pltpu.VMEM((512, 512), jnp.float32)],
        compiler_params=PARAMS,
    )(*values)


def place():
    row, col = lax.axis_index("row"), lax.axis_index("col")
    return row // 2, lax.rem(row, 2), col // 4, lax.rem(col, 4)


def choose(out_ref, take, yes_ref, no_ref):
    @pl.when(take)
    def _():
        out_ref[...] = yes_ref[...]

    @pl.when(jnp.logical_not(take))
    def _():
        out_ref[...] = no_ref[...]


def f32(*shape):
    return jax.ShapeDtypeStruct(shape, jnp.float32)


def local(kernel, values, outs, aliases={}):
    return pl.pallas_call(
        kernel,
        out_shape=outs,
        in_specs=[whole()] * len(values),
        out_specs=(whole(),) * len(outs),
        input_output_aliases=aliases,
        compiler_params=PARAMS,
    )(*values)


def pack_kernel(x_ref, low_ref, high_ref):
    def put(blocks):
        for at, (i, j) in enumerate(blocks):
            j = j % 2
            for p in range(16):
                part = low_ref if p < 8 else high_ref
                part[p % 8, at] = x_ref[i * B + p * 8 : i * B + p * 8 + 8, j * B : (j + 1) * B]

    @pl.when(lax.axis_index("col") == 0)
    def _():
        put(LEFT)

    @pl.when(lax.axis_index("col") > 0)
    def _():
        put(RIGHT)


def halve(take, got_ref, have_ref, low_ref, high_ref):
    n = low_ref.shape[0]
    choose(low_ref, take, got_ref.at[:n], have_ref.at[:n])
    choose(high_ref, take, got_ref.at[n:], have_ref.at[n:])


def core_kernel(have_ref, got_ref, low_ref, high_ref):
    halve(place()[1] == 1, got_ref, have_ref, low_ref, high_ref)


def y4_kernel(have_ref, got_ref, x_ref, far_ref, low_ref, high_ref, quarter_ref):
    y, core, z, xi = place()
    halve(y >= 4, got_ref, have_ref, low_ref, high_ref)
    choose(quarter_ref, xi >= 2, far_ref, x_ref.at[: 2 * B])


def y2_kernel(have_ref, got_ref, low_ref, high_ref):
    halve(lax.rem(place()[0] // 2, 2) == 1, got_ref, have_ref, low_ref, high_ref)


def y1_kernel(have_ref, got_ref, x_ref, down_ref, quarter_ref, far_ref, piece_ref, top_ref, quarter_out):
    y, core, z, xi = place()
    choose(quarter_out, z >= 4, far_ref, quarter_ref)
    choose(top_ref, y >= 4, down_ref, x_ref)
    holds = jnp.logical_and(z == 0, xi < 2)

    @pl.when(holds)
    def _():
        choose(piece_ref, lax.rem(y, 2) == 1, got_ref.at[0], have_ref.at[0])

    @pl.when(jnp.logical_not(holds))
    def _():
        piece_ref[...] = jnp.zeros_like(piece_ref)


def z_kernel(quarter_in, have_ref, got_ref, top_ref, down_ref, quarter_ref, piece_ref, top_out):
    del quarter_in, quarter_ref
    y, core, z, xi = place()
    choose(piece_ref, lax.rem(z, 2) == 1, got_ref, have_ref)
    choose(top_out, lax.rem(y // 2, 2) == 1, down_ref, top_ref)


def x_kernel(own_ref, o1_ref, o2_ref, o3_ref, quarter_ref, far_ref, top_ref, down_ref, both_ref, quarter_out, top_out):
    y, core, z, xi = place()
    sides = ((own_ref, o1_ref), (o1_ref, own_ref), (o2_ref, o3_ref), (o3_ref, o2_ref))
    for x, (left, right) in enumerate(sides):

        @pl.when(xi == x)
        def _(left=left, right=right):
            both_ref[:5] = left[...]
            both_ref[5:] = right[...]

    choose(quarter_out, lax.rem(z // 2, 2) == 1, far_ref, quarter_ref)
    choose(top_out, lax.rem(y, 2) == 1, down_ref, top_ref)


def gate_kernel(g_in, down_in, quarter_ref, far_ref, g_ref, down_ref, quarter_out):
    del g_in, down_in, g_ref, down_ref
    choose(quarter_out, lax.rem(place()[2], 2) == 1, far_ref, quarter_ref)


def mid_kernel(*refs):
    del refs


def on_device(x):
    zs, xs, ys = range(8), range(4), range(8)
    below, firsts = range(1, 16), range(2)

    def send(v, pairs):
        return lax.ppermute(v, ("row", "col"), [(32 * a + b, 32 * c + d) for (a, b), (c, d) in pairs])

    def along(v, pairs, rows=range(16)):
        return send(v, [((r, a), (r, b)) for r in rows for a, b in pairs])

    def across(v, pairs, cols=range(2, 32)):
        return send(v, [((a, c), (b, c)) for c in cols for a, b in pairs])

    def by_z(v, step):
        holders = range(0, 8, 2 * step)
        return along(v, [(4 * z + i, 4 * (z + step) + i) for z in holders for i in xs], below)

    def by_x(v, step):
        return along(v, [(4 * z + i, 4 * z + (i + step) % 4) for z in zs for i in xs], below)

    far = along(x[2 * B :], [(0, 3), (1, 2)], below)
    down = across(x, [(0, 8)])
    low, high = local(pack_kernel, (x,), (f32(8, 5, 8, B),) * 2)
    got = across(high, [(0, 1)], firsts)
    low, high = local(core_kernel, (low, got), (f32(4, 5, 8, B),) * 2)
    got = across(high, [(0, 8), (1, 9)], firsts)
    quarter = f32(2 * B, 2 * B)
    low, high, part = local(y4_kernel, (low, got, x, far), (f32(2, 5, 8, B),) * 2 + (quarter,))
    far = by_z(part, 4)
    got = across(high, [(0, 4), (1, 5), (8, 12), (9, 13)], firsts)
    low, high = local(y2_kernel, (low, got), (f32(1, 5, 8, B),) * 2)
    got = across(high, [(4 * q + k, 4 * q + k + 2) for q in range(4) for k in (0, 1)], firsts)
    piece, top, part = local(y1_kernel, (low, got, x, down, part, far), (f32(5, 8, B), f32(*x.shape), quarter))

    down = across(top, [(0, 4), (8, 12)])
    piece += sum(along(piece, [(0, 4 * z), (1, 4 * z + 1)]) for z in (4, 2, 6))
    got = along(piece, [(4 * z + i, 4 * z + 4 + i) for z in (0, 2, 4, 6) for i in (0, 1)])
    part, piece, top = local(
        z_kernel, (part, piece, got, top, down), (quarter, f32(5, 8, B), f32(*x.shape)), {0: 0}
    )
    others = [
        along(piece, [(4 * z + i, 4 * z + j) for z in zs for i, j in pairs])
        for pairs in (((0, 1), (1, 0)), ((0, 2), (1, 3)), ((0, 3), (1, 2)))
    ]
    far = by_z(part, 2)
    down = across(top, [(4 * q, 4 * q + 2) for q in range(4)])
    both, part, top = local(
        x_kernel, (piece, *others, part, far, top, down), (f32(10, 8, B), quarter, f32(*x.shape))
    )
    far = by_z(part, 1)
    down = across(top, [(2 * y, 2 * y + 1) for y in ys])
    gathered = lax.all_gather(both, "row")
    gathered, down, part = local(
        gate_kernel, (gathered, down, part, far), (f32(16, 10, 8, B), f32(*x.shape), quarter), {0: 0, 1: 1}
    )
    near, next_ = by_x(part, 1), by_x(part, 3)
    s, lower, inv = first_half(gathered, part)
    s, near, next_ = local(mid_kernel, (s, near, next_), (SQUARE, quarter, quarter), {0: 0, 1: 1, 2: 2})
    opposite = by_x(near, 1)
    _, lower, inv = second_half(s, lower, inv, near)
    return final(x, part, near, next_, opposite, top, down, lower, inv)


def solution(mesh):
    return jax.shard_map(
        on_device,
        mesh=mesh,
        in_specs=(P("row", "col"),),
        out_specs=(P(("row", "col"), None), P("row", "col")),
        check_vma=False,
    )
```

```python
import functools

import jax, jax.numpy as jnp
from jax import lax
from jax.experimental import pallas as pl
from jax.experimental.pallas import tpu as pltpu
from jax.sharding import PartitionSpec as P

HI = lax.Precision.HIGHEST
B = 128
S8 = 8

def rep(x):
    return jnp.broadcast_to(x, (S8, B))

def factor_tile(d_ref, m_ref, lt_ref):
    tiles = B // S8
    for b in range(tiles):
        rows = pl.ds(b * S8, S8)
        d = d_ref[rows, :]
        m = m_ref[rows, :]
        cols = [rep(d[:, b * S8 + k : b * S8 + k + 1]) for k in range(S8)]
        s = {}
        for i in range(S8):
            for k in range(i, S8):
                s[i, k] = rep(cols[k][i : i + 1, :])
        rd = [rep(d[j : j + 1, :]) for j in range(S8)]
        rm = [rep(m[j : j + 1, :]) for j in range(S8)]
        u, qd, qm, scale = {}, [], [], []
        for j in range(S8):
            inv = 1.0 / s[j, j]
            scale.append(lax.rsqrt(s[j, j]))
            for k in range(j + 1, S8):
                u[j, k] = s[j, k] * inv
            for i in range(j + 1, S8):
                for k in range(i, S8):
                    s[i, k] = s[i, k] - s[j, i] * u[j, k]
            qd.append(rd[j] * inv)
            qm.append(rm[j] * inv)
            for k in range(j + 1, S8):
                rd[k] = rd[k] - s[j, k] * qd[j]
                rm[k] = rm[k] - s[j, k] * qm[j]
        for t in range(b + 1, tiles):
            at = pl.ds(t * S8, S8)
            dt = d_ref[at, :]
            mt = m_ref[at, :]
            c = [rep(dt[:, b * S8 + k : b * S8 + k + 1]) for k in range(S8)]
            for j in range(S8):
                for k in range(j + 1, S8):
                    c[k] = c[k] - c[j] * u[j, k]
            for j in range(S8):
                dt = dt - c[j] * qd[j]
                mt = mt - c[j] * qm[j]
            d_ref[at, :] = dt
            m_ref[at, :] = mt
        sub = lax.broadcasted_iota(jnp.int32, (S8, B), 0)
        od, om = rd[0] * scale[0], rm[0] * scale[0]
        for j in range(1, S8):
            od = jnp.where(sub == j, rd[j] * scale[j], od)
            om = jnp.where(sub == j, rm[j] * scale[j], om)
        lt_ref[rows, :] = od
        m_ref[rows, :] = om

def dot(a, b, dims=((1,), (0,)), precision=HI):
    return lax.dot_general(a, b, (dims, ((), ())), precision=precision, preferred_element_type=jnp.float32)

N = 4 * B
LEFT = ((0, 0), (1, 0), (1, 1), (2, 0), (3, 0))
RIGHT = ((2, 2), (3, 2), (3, 3), (1, 2), (1, 3))


def eliminate(first, last, l_ref, inv_ref, s_ref, d_ref, m_ref, lt_ref):
    r128 = lax.broadcasted_iota(jnp.int32, (B, B), 0)
    c128 = lax.broadcasted_iota(jnp.int32, (B, B), 1)
    eye = jnp.where(r128 == c128, 1.0, 0.0).astype(jnp.float32)
    for k in range(first, last):
        lo, hi = k * B, (k + 1) * B
        d_ref[...] = s_ref[lo:hi, lo:hi]
        m_ref[...] = eye
        factor_tile(d_ref, m_ref, lt_ref)
        inv = m_ref[...]
        l_ref[lo:hi, lo:hi] = jnp.where(r128 >= c128, lt_ref[...].T, 0.0)
        inv_ref[lo:hi, lo:hi] = inv
        if k:
            inv_ref[lo:hi, :lo] = dot(inv, inv_ref[lo:hi, :lo])
        if hi < N:
            below = dot(s_ref[hi:, lo:hi], inv, ((1,), (1,)))
            l_ref[hi:, lo:hi] = below
            for i in range(k + 1, N // B):
                a, z = i * B, (i + 1) * B
                mine = below[a - hi : z - hi]
                s_ref[a:z, hi:z] -= dot(mine, below[: z - hi], ((1,), (1,)))
                inv_ref[a:z, :hi] -= dot(mine, inv_ref[lo:hi, :hi])


def first_kernel(g_ref, after_ref, s_ref, l_ref, inv_ref, d_ref, m_ref, lt_ref):
    del after_ref
    s_ref[...] = jnp.zeros((N, N), jnp.float32)
    for at, (i, j) in enumerate(LEFT + RIGHT):
        for r in range(16):
            p = (r % 2) * 8 + r // 2
            s_ref[i * B + p * 8 : i * B + p * 8 + 8, j * B : (j + 1) * B] = g_ref[r, at]
    for i, j in RIGHT[3:]:
        s_ref[j * B : (j + 1) * B, i * B : (i + 1) * B] = s_ref[i * B : (i + 1) * B, j * B : (j + 1) * B].T
    inv_ref[...] = jnp.zeros((N, N), jnp.float32)
    l_ref[...] = jnp.zeros((N, N), jnp.float32)
    eliminate(0, 2, l_ref, inv_ref, s_ref, d_ref, m_ref, lt_ref)


def second_kernel(s_in, l_in, inv_in, after_ref, s_ref, l_ref, inv_ref, d_ref, m_ref, lt_ref):
    del s_in, l_in, inv_in, after_ref
    eliminate(2, 4, l_ref, inv_ref, s_ref, d_ref, m_ref, lt_ref)


def whole():
    return pl.BlockSpec(memory_space=pltpu.VMEM)


def anywhere():
    return pl.BlockSpec(memory_space=pl.ANY)


PARAMS = pltpu.CompilerParams(vmem_limit_bytes=40 * 2**20)
SQUARE = jax.ShapeDtypeStruct((N, N), jnp.float32)


def first_half(gathered, after):
    return pl.pallas_call(
        first_kernel,
        out_shape=(SQUARE,) * 3,
        in_specs=[whole(), anywhere()],
        out_specs=(whole(),) * 3,
        scratch_shapes=[pltpu.VMEM((B, B), jnp.float32)] * 3,
        compiler_params=PARAMS,
    )(gathered, after)


def second_half(s, lower, inv, after):
    return pl.pallas_call(
        second_kernel,
        out_shape=(SQUARE,) * 3,
        in_specs=[whole()] * 3 + [anywhere()],
        out_specs=(whole(),) * 3,
        input_output_aliases={0: 0, 1: 1, 2: 2},
        scratch_shapes=[pltpu.VMEM((B, B), jnp.float32)] * 3,
        compiler_params=PARAMS,
    )(s, lower, inv, after)


def final_kernel(x_ref, q0_ref, q1_ref, q2_ref, q3_ref, top_ref, far_ref, l_ref, inv_ref, panel_ref, out_ref, u_ref, f_ref):
    row, col = lax.axis_index("row"), lax.axis_index("col")
    inv = inv_ref[...]
    half = 2 * B

    def solve_top(ref):
        u_ref[:half] = dot(inv[:half, :half], ref[:half])
        u_ref[half:] = dot(inv[half:], ref[...])

    @pl.when(lax.rem(row, 2) == 0)
    def _():
        solve_top(top_ref)

    @pl.when(lax.rem(row, 2) == 1)
    def _():
        solve_top(far_ref)

    @pl.when(row == 0)
    def _():
        f_ref[...] = l_ref[...]

    for x in range(4):

        @pl.when(jnp.logical_and(row > 0, lax.rem(col, 4) == x))
        def _(x=x):
            held = {x: q0_ref, (x + 3) % 4: q1_ref, (x + 1) % 4: q2_ref, (x + 2) % 4: q3_ref}
            for lo, left, right in ((0, held[0], held[1]), (half, held[3], held[2])):
                f_ref[lo : lo + half, :half] = dot(left[...], inv[:half, :half], ((1,), (1,)))
                f_ref[lo : lo + half, half:] = dot(left[...], inv[half:, :half], ((1,), (1,))) + dot(
                    right[...], inv[half:, half:], ((1,), (1,))
                )

    panel_ref[...] = f_ref[pl.ds(pl.multiple_of(col * 16, 16), 16), :]
    live = jnp.logical_and(row > 0, col > 1)

    @pl.when(live)
    def _():
        out_ref[...] = x_ref[...] - lax.dot_general(
            f_ref[...],
            u_ref[...],
            (((1,), (0,)), ((), ())),
            precision=lax.Precision.HIGH,
            preferred_element_type=jnp.float32,
        )

    @pl.when(jnp.logical_not(live))
    def _():
        out_ref[...] = jnp.zeros_like(out_ref)


def final(*values):
    return pl.pallas_call(
        final_kernel,
        out_shape=(
            jax.ShapeDtypeStruct((16, 512), jnp.float32),
            jax.ShapeDtypeStruct((512, 256), jnp.float32),
        ),
        in_specs=[whole()] * 9,
        out_specs=(whole(), whole()),
        scratch_shapes=[pltpu.VMEM((512, 256), jnp.float32), pltpu.VMEM((512, 512), jnp.float32)],
        compiler_params=PARAMS,
    )(*values)


def place():
    row, col = lax.axis_index("row"), lax.axis_index("col")
    return row // 2, lax.rem(row, 2), col // 4, lax.rem(col, 4)


def choose(out_ref, take, yes_ref, no_ref):
    @pl.when(take)
    def _():
        out_ref[...] = yes_ref[...]

    @pl.when(jnp.logical_not(take))
    def _():
        out_ref[...] = no_ref[...]


def f32(*shape):
    return jax.ShapeDtypeStruct(shape, jnp.float32)


def local(kernel, values, outs, aliases={}):
    return pl.pallas_call(
        kernel,
        out_shape=outs,
        in_specs=[whole()] * len(values),
        out_specs=(whole(),) * len(outs),
        input_output_aliases=aliases,
        compiler_params=PARAMS,
    )(*values)


def pack_kernel(x_ref, low_ref, high_ref):
    def put(blocks):
        for at, (i, j) in enumerate(blocks):
            j = j % 2
            for p in range(16):
                part = low_ref if p < 8 else high_ref
                part[p % 8, at] = x_ref[i * B + p * 8 : i * B + p * 8 + 8, j * B : (j + 1) * B]

    @pl.when(lax.axis_index("col") == 0)
    def _():
        put(LEFT)

    @pl.when(lax.axis_index("col") > 0)
    def _():
        put(RIGHT)


def halve(take, got_ref, have_ref, low_ref, high_ref):
    n = low_ref.shape[0]
    choose(low_ref, take, got_ref.at[:n], have_ref.at[:n])
    choose(high_ref, take, got_ref.at[n:], have_ref.at[n:])


def core_kernel(have_ref, got_ref, low_ref, high_ref):
    halve(place()[1] == 1, got_ref, have_ref, low_ref, high_ref)


def y4_kernel(have_ref, got_ref, x_ref, far_ref, low_ref, high_ref, quarter_ref):
    y, core, z, xi = place()
    halve(y >= 4, got_ref, have_ref, low_ref, high_ref)
    choose(quarter_ref, xi >= 2, far_ref, x_ref.at[: 2 * B])


def y2_kernel(have_ref, got_ref, low_ref, high_ref):
    halve(lax.rem(place()[0] // 2, 2) == 1, got_ref, have_ref, low_ref, high_ref)


def y1_kernel(have_ref, got_ref, x_ref, down_ref, quarter_ref, far_ref, piece_ref, top_ref, quarter_out):
    y, core, z, xi = place()
    choose(quarter_out, z >= 4, far_ref, quarter_ref)
    choose(top_ref, y >= 4, down_ref, x_ref)
    holds = jnp.logical_and(z == 0, xi < 2)

    @pl.when(holds)
    def _():
        choose(piece_ref, lax.rem(y, 2) == 1, got_ref.at[0], have_ref.at[0])

    @pl.when(jnp.logical_not(holds))
    def _():
        piece_ref[...] = jnp.zeros_like(piece_ref)


def z_kernel(quarter_in, have_ref, got_ref, late_ref, top_ref, down_ref, quarter_ref, piece_ref, top_out):
    del quarter_in, quarter_ref
    y, core, z, xi = place()
    late = jnp.logical_or(z == 4, z == 5)
    soon = jnp.logical_and(lax.rem(z, 2) == 1, z != 5)

    @pl.when(late)
    def _():
        piece_ref[...] = late_ref[...]

    @pl.when(jnp.logical_not(late))
    def _():
        choose(piece_ref, soon, got_ref, have_ref)

    choose(top_out, lax.rem(y // 2, 2) == 1, down_ref, top_ref)


def x_kernel(own_ref, o1_ref, o2_ref, o3_ref, quarter_ref, far_ref, top_ref, down_ref, both_ref, quarter_out, top_out):
    y, core, z, xi = place()
    sides = ((own_ref, o1_ref), (o1_ref, own_ref), (o2_ref, o3_ref), (o3_ref, o2_ref))
    for x, (left, right) in enumerate(sides):

        @pl.when(xi == x)
        def _(left=left, right=right):
            both_ref[:5] = left[...]
            both_ref[5:] = right[...]

    choose(quarter_out, lax.rem(z // 2, 2) == 1, far_ref, quarter_ref)
    choose(top_out, lax.rem(y, 2) == 1, down_ref, top_ref)


def gate_kernel(g_in, down_in, quarter_ref, far_ref, g_ref, down_ref, quarter_out):
    del g_in, down_in, g_ref, down_ref
    choose(quarter_out, lax.rem(place()[2], 2) == 1, far_ref, quarter_ref)


def mid_kernel(*refs):
    del refs


def on_device(x):
    zs, xs, ys = range(8), range(4), range(8)
    below, firsts = range(1, 16), range(2)

    def send(v, pairs):
        return lax.ppermute(v, ("row", "col"), [(32 * a + b, 32 * c + d) for (a, b), (c, d) in pairs])

    def along(v, pairs, rows=range(16)):
        return send(v, [((r, a), (r, b)) for r in rows for a, b in pairs])

    def across(v, pairs, cols=range(2, 32)):
        return send(v, [((a, c), (b, c)) for c in cols for a, b in pairs])

    def by_z(v, step):
        holders = range(0, 8, 2 * step)
        return along(v, [(4 * z + i, 4 * (z + step) + i) for z in holders for i in xs], below)

    def by_x(v, step):
        return along(v, [(4 * z + i, 4 * z + (i + step) % 4) for z in zs for i in xs], below)

    far = along(x[2 * B :], [(0, 3), (1, 2)], below)
    down = across(x, [(0, 8)])
    low, high = local(pack_kernel, (x,), (f32(8, 5, 8, B),) * 2)
    got = across(high, [(0, 1)], firsts)
    low, high = local(core_kernel, (low, got), (f32(4, 5, 8, B),) * 2)
    got = across(high, [(0, 8), (1, 9)], firsts)
    quarter = f32(2 * B, 2 * B)
    low, high, part = local(y4_kernel, (low, got, x, far), (f32(2, 5, 8, B),) * 2 + (quarter,))
    far = by_z(part, 4)
    got = across(high, [(0, 4), (1, 5), (8, 12), (9, 13)], firsts)
    low, high = local(y2_kernel, (low, got), (f32(1, 5, 8, B),) * 2)
    got = across(high, [(4 * q + k, 4 * q + k + 2) for q in range(4) for k in (0, 1)], firsts)
    piece, top, part = local(y1_kernel, (low, got, x, down, part, far), (f32(5, 8, B), f32(*x.shape), quarter))

    down = across(top, [(0, 4), (8, 12)])
    piece += sum(along(piece, [(0, 4 * z), (1, 4 * z + 1)]) for z in (2, 6))
    got = [
        along(piece, [(4 * a + i, 4 * b + i) for a, b in pairs for i in (0, 1)])
        for pairs in (((0, 1), (2, 3), (6, 7)), ((0, 4), (6, 5)))
    ]
    part, piece, top = local(
        z_kernel, (part, piece, *got, top, down), (quarter, f32(5, 8, B), f32(*x.shape)), {0: 0}
    )
    others = [
        along(piece, [(4 * z + i, 4 * z + j) for z in zs for i, j in pairs])
        for pairs in (((0, 1), (1, 0)), ((0, 2), (1, 3)), ((0, 3), (1, 2)))
    ]
    far = by_z(part, 2)
    down = across(top, [(4 * q, 4 * q + 2) for q in range(4)])
    both, part, top = local(
        x_kernel, (piece, *others, part, far, top, down), (f32(10, 8, B), quarter, f32(*x.shape))
    )
    far = by_z(part, 1)
    down = across(top, [(2 * y, 2 * y + 1) for y in ys])
    gathered = lax.all_gather(both, "row")
    gathered, down, part = local(
        gate_kernel, (gathered, down, part, far), (f32(16, 10, 8, B), f32(*x.shape), quarter), {0: 0, 1: 1}
    )
    near, next_ = by_x(part, 1), by_x(part, 3)
    s, lower, inv = first_half(gathered, part)
    s, near = local(mid_kernel, (s, near), (SQUARE, quarter), {0: 0, 1: 1})
    opposite = by_x(near, 1)
    _, lower, inv = second_half(s, lower, inv, near)
    return final(x, part, near, next_, opposite, top, down, lower, inv)


def solution(mesh):
    return jax.shard_map(
        on_device,
        mesh=mesh,
        in_specs=(P("row", "col"),),
        out_specs=(P(("row", "col"), None), P("row", "col")),
        check_vma=False,
    )
```

```python
import functools

import jax, jax.numpy as jnp
from jax import lax
from jax.experimental import pallas as pl
from jax.experimental.pallas import tpu as pltpu
from jax.sharding import PartitionSpec as P

HI = lax.Precision.HIGHEST
B = 128
S8 = 8

def rep(x):
    return jnp.broadcast_to(x, (S8, B))

def factor_tile(d_ref, m_ref, lt_ref):
    tiles = B // S8
    for b in range(tiles):
        rows = pl.ds(b * S8, S8)
        d = d_ref[rows, :]
        m = m_ref[rows, :]
        cols = [rep(d[:, b * S8 + k : b * S8 + k + 1]) for k in range(S8)]
        s = {}
        for i in range(S8):
            for k in range(i, S8):
                s[i, k] = rep(cols[k][i : i + 1, :])
        rd = [rep(d[j : j + 1, :]) for j in range(S8)]
        rm = [rep(m[j : j + 1, :]) for j in range(S8)]
        u, qd, qm, scale = {}, [], [], []
        for j in range(S8):
            inv = 1.0 / s[j, j]
            scale.append(lax.rsqrt(s[j, j]))
            for k in range(j + 1, S8):
                u[j, k] = s[j, k] * inv
            for i in range(j + 1, S8):
                for k in range(i, S8):
                    s[i, k] = s[i, k] - s[j, i] * u[j, k]
            qd.append(rd[j] * inv)
            qm.append(rm[j] * inv)
            for k in range(j + 1, S8):
                rd[k] = rd[k] - s[j, k] * qd[j]
                rm[k] = rm[k] - s[j, k] * qm[j]
        for t in range(b + 1, tiles):
            at = pl.ds(t * S8, S8)
            dt = d_ref[at, :]
            mt = m_ref[at, :]
            c = [rep(dt[:, b * S8 + k : b * S8 + k + 1]) for k in range(S8)]
            for j in range(S8):
                for k in range(j + 1, S8):
                    c[k] = c[k] - c[j] * u[j, k]
            for j in range(S8):
                dt = dt - c[j] * qd[j]
                mt = mt - c[j] * qm[j]
            d_ref[at, :] = dt
            m_ref[at, :] = mt
        sub = lax.broadcasted_iota(jnp.int32, (S8, B), 0)
        od, om = rd[0] * scale[0], rm[0] * scale[0]
        for j in range(1, S8):
            od = jnp.where(sub == j, rd[j] * scale[j], od)
            om = jnp.where(sub == j, rm[j] * scale[j], om)
        lt_ref[rows, :] = od
        m_ref[rows, :] = om

def dot(a, b, dims=((1,), (0,)), precision=HI):
    return lax.dot_general(a, b, (dims, ((), ())), precision=precision, preferred_element_type=jnp.float32)

N = 4 * B
LEFT = ((0, 0), (1, 0), (1, 1), (2, 0), (3, 0))
RIGHT = ((2, 2), (3, 2), (3, 3), (1, 2), (1, 3))


def eliminate(first, last, l_ref, inv_ref, s_ref, d_ref, m_ref, lt_ref):
    r128 = lax.broadcasted_iota(jnp.int32, (B, B), 0)
    c128 = lax.broadcasted_iota(jnp.int32, (B, B), 1)
    eye = jnp.where(r128 == c128, 1.0, 0.0).astype(jnp.float32)
    for k in range(first, last):
        lo, hi = k * B, (k + 1) * B
        d_ref[...] = s_ref[lo:hi, lo:hi]
        m_ref[...] = eye
        factor_tile(d_ref, m_ref, lt_ref)
        inv = m_ref[...]
        l_ref[lo:hi, lo:hi] = jnp.where(r128 >= c128, lt_ref[...].T, 0.0)
        inv_ref[lo:hi, lo:hi] = inv
        if k:
            inv_ref[lo:hi, :lo] = dot(inv, inv_ref[lo:hi, :lo])
        if hi < N:
            below = dot(s_ref[hi:, lo:hi], inv, ((1,), (1,)))
            l_ref[hi:, lo:hi] = below
            for i in range(k + 1, N // B):
                a, z = i * B, (i + 1) * B
                mine = below[a - hi : z - hi]
                s_ref[a:z, hi:z] -= dot(mine, below[: z - hi], ((1,), (1,)))
                inv_ref[a:z, :hi] -= dot(mine, inv_ref[lo:hi, :hi])


def first_kernel(g_ref, after_ref, s_ref, l_ref, inv_ref, d_ref, m_ref, lt_ref):
    del after_ref
    s_ref[...] = jnp.zeros((N, N), jnp.float32)
    for at, (i, j) in enumerate(LEFT + RIGHT):
        for r in range(16):
            p = (r % 2) * 8 + r // 2
            s_ref[i * B + p * 8 : i * B + p * 8 + 8, j * B : (j + 1) * B] = g_ref[r, at]
    for i, j in RIGHT[3:]:
        s_ref[j * B : (j + 1) * B, i * B : (i + 1) * B] = s_ref[i * B : (i + 1) * B, j * B : (j + 1) * B].T
    inv_ref[...] = jnp.zeros((N, N), jnp.float32)
    l_ref[...] = jnp.zeros((N, N), jnp.float32)
    eliminate(0, 2, l_ref, inv_ref, s_ref, d_ref, m_ref, lt_ref)


def second_kernel(s_in, l_in, inv_in, after_ref, s_ref, l_ref, inv_ref, d_ref, m_ref, lt_ref):
    del s_in, l_in, inv_in, after_ref
    eliminate(2, 4, l_ref, inv_ref, s_ref, d_ref, m_ref, lt_ref)


def whole():
    return pl.BlockSpec(memory_space=pltpu.VMEM)


def anywhere():
    return pl.BlockSpec(memory_space=pl.ANY)


PARAMS = pltpu.CompilerParams(vmem_limit_bytes=40 * 2**20)
SQUARE = jax.ShapeDtypeStruct((N, N), jnp.float32)


def first_half(gathered, after):
    return pl.pallas_call(
        first_kernel,
        out_shape=(SQUARE,) * 3,
        in_specs=[whole(), anywhere()],
        out_specs=(whole(),) * 3,
        scratch_shapes=[pltpu.VMEM((B, B), jnp.float32)] * 3,
        compiler_params=PARAMS,
    )(gathered, after)


def second_half(s, lower, inv, after):
    return pl.pallas_call(
        second_kernel,
        out_shape=(SQUARE,) * 3,
        in_specs=[whole()] * 3 + [anywhere()],
        out_specs=(whole(),) * 3,
        input_output_aliases={0: 0, 1: 1, 2: 2},
        scratch_shapes=[pltpu.VMEM((B, B), jnp.float32)] * 3,
        compiler_params=PARAMS,
    )(s, lower, inv, after)


def final_kernel(x_ref, q0_ref, q1_ref, q2_ref, q3_ref, top_ref, far_ref, l_ref, inv_ref, panel_ref, out_ref, u_ref, f_ref):
    row, col = lax.axis_index("row"), lax.axis_index("col")
    inv = inv_ref[...]
    half = 2 * B

    def solve_top(ref):
        u_ref[:half] = dot(inv[:half, :half], ref[:half])
        u_ref[half:] = dot(inv[half:], ref[...])

    @pl.when(lax.rem(row, 2) == 0)
    def _():
        solve_top(top_ref)

    @pl.when(lax.rem(row, 2) == 1)
    def _():
        solve_top(far_ref)

    @pl.when(row == 0)
    def _():
        f_ref[...] = l_ref[...]

    for x in range(4):

        @pl.when(jnp.logical_and(row > 0, lax.rem(col, 4) == x))
        def _(x=x):
            held = {x: q0_ref, (x + 3) % 4: q1_ref, (x + 1) % 4: q2_ref, (x + 2) % 4: q3_ref}
            for lo, left, right in ((0, held[0], held[1]), (half, held[3], held[2])):
                f_ref[lo : lo + half, :half] = dot(left[...], inv[:half, :half], ((1,), (1,)))
                f_ref[lo : lo + half, half:] = dot(left[...], inv[half:, :half], ((1,), (1,))) + dot(
                    right[...], inv[half:, half:], ((1,), (1,))
                )

    panel_ref[...] = f_ref[pl.ds(pl.multiple_of(col * 16, 16), 16), :]
    live = jnp.logical_and(row > 0, col > 1)

    @pl.when(live)
    def _():
        out_ref[...] = x_ref[...] - lax.dot_general(
            f_ref[...],
            u_ref[...],
            (((1,), (0,)), ((), ())),
            precision=lax.Precision.HIGH,
            preferred_element_type=jnp.float32,
        )

    @pl.when(jnp.logical_not(live))
    def _():
        out_ref[...] = jnp.zeros_like(out_ref)


def final(*values):
    return pl.pallas_call(
        final_kernel,
        out_shape=(
            jax.ShapeDtypeStruct((16, 512), jnp.float32),
            jax.ShapeDtypeStruct((512, 256), jnp.float32),
        ),
        in_specs=[whole()] * 9,
        out_specs=(whole(), whole()),
        scratch_shapes=[pltpu.VMEM((512, 256), jnp.float32), pltpu.VMEM((512, 512), jnp.float32)],
        compiler_params=PARAMS,
    )(*values)


def place():
    row, col = lax.axis_index("row"), lax.axis_index("col")
    return row // 2, lax.rem(row, 2), col // 4, lax.rem(col, 4)


def choose(out_ref, take, yes_ref, no_ref):
    @pl.when(take)
    def _():
        out_ref[...] = yes_ref[...]

    @pl.when(jnp.logical_not(take))
    def _():
        out_ref[...] = no_ref[...]


def f32(*shape):
    return jax.ShapeDtypeStruct(shape, jnp.float32)


def local(kernel, values, outs, aliases={}):
    return pl.pallas_call(
        kernel,
        out_shape=outs,
        in_specs=[whole()] * len(values),
        out_specs=(whole(),) * len(outs),
        input_output_aliases=aliases,
        compiler_params=PARAMS,
    )(*values)


def pack_kernel(x_ref, low_ref, high_ref):
    def put(blocks):
        for at, (i, j) in enumerate(blocks):
            j = j % 2
            for p in range(16):
                part = low_ref if p < 8 else high_ref
                part[p % 8, at] = x_ref[i * B + p * 8 : i * B + p * 8 + 8, j * B : (j + 1) * B]

    @pl.when(lax.axis_index("col") == 0)
    def _():
        put(LEFT)

    @pl.when(lax.axis_index("col") > 0)
    def _():
        put(RIGHT)


def halve(take, got_ref, have_ref, low_ref, high_ref):
    n = low_ref.shape[0]
    choose(low_ref, take, got_ref.at[:n], have_ref.at[:n])
    choose(high_ref, take, got_ref.at[n:], have_ref.at[n:])


def core_kernel(have_ref, got_ref, low_ref, high_ref):
    halve(place()[1] == 1, got_ref, have_ref, low_ref, high_ref)


def y4_kernel(have_ref, got_ref, x_ref, far_ref, low_ref, high_ref, quarter_ref):
    y, core, z, xi = place()
    halve(y >= 4, got_ref, have_ref, low_ref, high_ref)
    choose(quarter_ref, xi >= 2, far_ref, x_ref.at[: 2 * B])


def y2_kernel(have_ref, got_ref, low_ref, high_ref):
    halve(lax.rem(place()[0] // 2, 2) == 1, got_ref, have_ref, low_ref, high_ref)


def y1_kernel(have_ref, got_ref, x_ref, down_ref, quarter_ref, far_ref, piece_ref, top_ref, quarter_out):
    y, core, z, xi = place()
    choose(quarter_out, z >= 4, far_ref, quarter_ref)
    choose(top_ref, y >= 4, down_ref, x_ref)
    holds = jnp.logical_and(z == 0, xi < 2)

    @pl.when(holds)
    def _():
        choose(piece_ref, lax.rem(y, 2) == 1, got_ref.at[0], have_ref.at[0])

    @pl.when(jnp.logical_not(holds))
    def _():
        piece_ref[...] = jnp.zeros_like(piece_ref)


def z_kernel(quarter_in, have_ref, got_ref, late_ref, top_ref, down_ref, quarter_ref, piece_ref, top_out):
    del quarter_in, quarter_ref
    y, core, z, xi = place()
    late = jnp.logical_or(z == 4, z == 5)
    soon = jnp.logical_and(lax.rem(z, 2) == 1, z != 5)

    @pl.when(late)
    def _():
        piece_ref[...] = late_ref[...]

    @pl.when(jnp.logical_not(late))
    def _():
        choose(piece_ref, soon, got_ref, have_ref)

    choose(top_out, lax.rem(y // 2, 2) == 1, down_ref, top_ref)


def x_kernel(own_ref, o1_ref, o2_ref, o3_ref, quarter_ref, far_ref, top_ref, down_ref, both_ref, quarter_out, top_out):
    y, core, z, xi = place()
    sides = ((own_ref, o1_ref), (o1_ref, own_ref), (o2_ref, o3_ref), (o3_ref, o2_ref))
    for x, (left, right) in enumerate(sides):

        @pl.when(xi == x)
        def _(left=left, right=right):
            both_ref[:5] = left[...]
            both_ref[5:] = right[...]

    choose(quarter_out, lax.rem(z // 2, 2) == 1, far_ref, quarter_ref)
    choose(top_out, lax.rem(y, 2) == 1, down_ref, top_ref)


def gate_kernel(g_in, down_in, quarter_ref, far_ref, g_ref, down_ref, quarter_out):
    del g_in, down_in, g_ref, down_ref
    choose(quarter_out, lax.rem(place()[2], 2) == 1, far_ref, quarter_ref)


def mid_kernel(*refs):
    del refs


def on_device(x):
    zs, xs, ys = range(8), range(4), range(8)
    below, firsts = range(1, 16), range(2)

    def send(v, pairs):
        return lax.ppermute(v, ("row", "col"), [(32 * a + b, 32 * c + d) for (a, b), (c, d) in pairs])

    def along(v, pairs, rows=range(16)):
        return send(v, [((r, a), (r, b)) for r in rows for a, b in pairs])

    def across(v, pairs, cols=range(2, 32)):
        return send(v, [((a, c), (b, c)) for c in cols for a, b in pairs])

    def by_z(v, step):
        holders = range(0, 8, 2 * step)
        return along(v, [(4 * z + i, 4 * (z + step) + i) for z in holders for i in xs], below)

    def by_x(v, step):
        return along(v, [(4 * z + i, 4 * z + (i + step) % 4) for z in zs for i in xs], below)

    far = along(x[2 * B :], [(0, 3), (1, 2)], below)
    down = across(x, [(0, 8)])
    low, high = local(pack_kernel, (x,), (f32(8, 5, 8, B),) * 2)
    got = across(high, [(0, 1)], firsts)
    low, high = local(core_kernel, (low, got), (f32(4, 5, 8, B),) * 2)
    got = across(high, [(0, 8), (1, 9)], firsts)
    quarter = f32(2 * B, 2 * B)
    low, high, part = local(y4_kernel, (low, got, x, far), (f32(2, 5, 8, B),) * 2 + (quarter,))
    far = by_z(part, 4)
    got = across(high, [(0, 4), (1, 5), (8, 12), (9, 13)], firsts)
    low, high = local(y2_kernel, (low, got), (f32(1, 5, 8, B),) * 2)
    got = across(high, [(4 * q + k, 4 * q + k + 2) for q in range(4) for k in (0, 1)], firsts)
    piece, top, part = local(y1_kernel, (low, got, x, down, part, far), (f32(5, 8, B), f32(*x.shape), quarter))

    down = across(top, [(0, 4), (8, 12)])
    piece += sum(along(piece, [(0, 4 * z), (1, 4 * z + 1)]) for z in (2, 6))
    got = [
        along(piece, [(4 * a + i, 4 * b + i) for a, b in pairs for i in (0, 1)])
        for pairs in (((0, 1), (2, 3), (6, 7)), ((0, 4), (6, 5)))
    ]
    part, piece, top = local(
        z_kernel, (part, piece, *got, top, down), (quarter, f32(5, 8, B), f32(*x.shape)), {0: 0}
    )
    others = [
        along(piece, [(4 * z + i, 4 * z + j) for z in zs for i, j in pairs])
        for pairs in (((0, 1), (1, 0)), ((0, 2), (1, 3)), ((0, 3), (1, 2)))
    ]
    far = by_z(part, 2)
    down = across(top, [(4 * q, 4 * q + 2) for q in range(4)])
    both, part, top = local(
        x_kernel, (piece, *others, part, far, top, down), (f32(10, 8, B), quarter, f32(*x.shape))
    )
    far = by_z(part, 1)
    down = across(top, [(2 * y, 2 * y + 1) for y in ys])
    gathered = lax.all_gather(both, "row")
    gathered, down, part = local(
        gate_kernel, (gathered, down, part, far), (f32(16, 10, 8, B), f32(*x.shape), quarter), {0: 0, 1: 1}
    )
    near = by_x(part, 1)
    s, lower, inv = first_half(gathered, part)
    s, near, part = local(mid_kernel, (s, near, part), (SQUARE, quarter, quarter), {0: 0, 1: 1, 2: 2})
    next_ = by_x(part, 3)
    opposite = by_x(near, 1)
    _, lower, inv = second_half(s, lower, inv, near)
    return final(x, part, near, next_, opposite, top, down, lower, inv)


def solution(mesh):
    return jax.shard_map(
        on_device,
        mesh=mesh,
        in_specs=(P("row", "col"),),
        out_specs=(P(("row", "col"), None), P("row", "col")),
        check_vma=False,
    )
```
